128 devices in a mesh: ty: 4 (over z_lo, core), tx: 32 (over y, x, z_hi).
Axes of the slice: x: 4, y: 4, z: 4 (z_hi: 2, z_lo: 2; z = z_hi * 2 + z_lo), core: 2. Of those that a mesh axis runs over, the one named last changes fastest.
Arguments:
- out_grad: bfloat16 [2, 128, 512, 192], P(None, 'ty', 'tx'), may hold values from -6 to 6
- preact: bfloat16 [2, 64, 256, 384], P(None, 'ty', 'tx'), may hold values from -8 to 8
- norm_gain: float32 [384], replicated, may hold values from 0.5 to 2
- mid_weight: bfloat16 [3, 3, 3, 384, 384], replicated, may hold values from -0.0625 to 0.0625
- up_weight: bfloat16 [3, 3, 3, 384, 192], replicated, may hold values from -0.078125 to 0.078125
- patch_weight: bfloat16 [3072, 2560], P(None, 'ty'), may hold values from -0.109375 to 0.109375
- query_proj: bfloat16 [4096, 2560], P('tx', 'ty'), may hold values from -4.6 to 4.6
- key_proj: bfloat16 [4096, 2560], P('tx', 'ty'), may hold values from -4.6 to 4.6
- value_proj: bfloat16 [4096, 2560], P('tx', 'ty'), may hold values from -6 to 6
- qkv_weight: bfloat16 [5120, 3, 2560], P('tx', None, 'ty'), may hold values from -0.0625 to 0.0625
Outputs:
- feature_grad: bfloat16 [2, 64, 256, 384], P(None, 'ty', 'tx')
- latent_grad: bfloat16 [4096, 5120], P('tx', 'ty')
The draws below stay inside these ranges and needn't reach their ends.
All inputs are finite; a program needn't handle non-finite values.
Results may differ from the reference program's by a relative error of at most 0.03.
Values may be sent and summed in bfloat16 or wider, within the bound.
A program may use at most 192 MiB of HBM per device.

```python
import math
import jax
import jax.numpy as jnp
from jax import lax

MID_CH = 384
OUT_CH = 192
FRAMES = 2
ROWS_DEV = 16
COLS_DEV = 8
IMG_ROWS = 64
IMG_COLS = 256
FINE_ROWS = 128
FINE_COLS = 512
WIDTH = 5120
HEADS = 20
HEAD_DIM = 128
TOK_DEV = 128
TOKENS = 4096
N_TY = 4
N_TX = 32


def draw_key_proj(key, part):
    key = jax.random.fold_in(key, 1)
    values = jax.random.truncated_normal(key, -4.6, 4.6, (TOKENS, HEADS * HEAD_DIM), jnp.float32)
    return values.astype(jnp.bfloat16)


def draw_query_proj(key, part):
    key = jax.random.fold_in(key, 2)
    values = jax.random.truncated_normal(key, -4.6, 4.6, (TOKENS, HEADS * HEAD_DIM), jnp.float32)
    return values.astype(jnp.bfloat16)


def shard_levels(rng, dims, cuts, smallest, high):
    gain = 1.0
    for position, blocks in cuts:
        steps = jax.random.uniform(jax.random.fold_in(jax.random.fold_in(rng, 6), position), (blocks,), jnp.float32, smallest / len(cuts), high / len(cuts))
        gain = gain * jnp.repeat(jnp.exp(steps), dims[position] // blocks).reshape((-1,) + (1,) * (len(dims) - 1 - position))
    return gain


def centred(own_key, shape, width, limit, cuts=(), kind=jnp.bfloat16):
    drawn = jax.random.normal(own_key, shape, jnp.float32) * width
    if len(cuts) > 0:
        drawn = shard_levels(own_key, shape, cuts, -0.22, 0.18) * drawn
    return jnp.clip(drawn, min=-limit, max=limit).astype(kind)


def setup_inputs(seed: int = 0) -> dict:
    seeds = jax.random.split(jax.random.key(seed), 11)
    return {
        "out_grad": centred(seeds[0], (FRAMES, FINE_ROWS, FINE_COLS, OUT_CH), 1.0, 6.0, ((1, 4), (2, 32))),
        "preact": centred(seeds[1], (FRAMES, IMG_ROWS, IMG_COLS, MID_CH), 2.0, 8.0, ((1, 4), (2, 32))),
        "norm_gain": jnp.clip(jnp.exp(jax.random.uniform(seeds[2], (MID_CH,), jnp.float32, math.log(0.5), math.log(2.0))), 0.5, 2.0),
        "mid_weight": centred(seeds[3], (3, 3, 3, MID_CH, MID_CH), (27 * MID_CH) ** -0.5, 0.0625),
        "up_weight": centred(seeds[4], (3, 3, 3, MID_CH, OUT_CH), (27 * OUT_CH) ** -0.5, 0.078125),
        "patch_weight": centred(seeds[5], (4 * FRAMES * MID_CH, HEADS * HEAD_DIM), (4 * FRAMES * MID_CH) ** -0.5, 0.109375, ((1, 4),)),
        "query_proj": draw_query_proj(jax.random.fold_in(seeds[10], 71), 0),
        "key_proj": draw_key_proj(jax.random.fold_in(seeds[10], 71), 0),
        "value_proj": centred(seeds[8], (TOKENS, HEADS * HEAD_DIM), 1.0, 6.0, ((0, 32), (1, 4))),
        "qkv_weight": centred(seeds[9], (WIDTH, 3, HEADS * HEAD_DIM), (3 * HEADS * HEAD_DIM) ** -0.5, 0.0625, ((0, 32), (2, 4))),
    }


def transpose_conv(padded, weight):
    frames = padded.shape[0]
    out_rows = padded.shape[1] - 2
    out_cols = padded.shape[2] - 2
    extended = jnp.pad(padded, ((0, 2), (0, 0), (0, 0), (0, 0)))
    in_ch = weight.shape[3]
    out_ch = weight.shape[4]
    summed = jnp.zeros((frames * out_rows * out_cols, in_ch), jnp.float32)
    for tap_time in range(3):
        for tap_row in range(3):
            for tap_col in range(3):
                portion = extended[2 - tap_time:2 - tap_time + frames, 2 - tap_row:2 - tap_row + out_rows, 2 - tap_col:2 - tap_col + out_cols]
                summed = summed + jnp.dot(portion.reshape(-1, out_ch), weight[tap_time, tap_row, tap_col].T, preferred_element_type=jnp.float32)
    return summed.reshape(frames, out_rows, out_cols, in_ch)


def pool_pairs(grid):
    frames, rows, cols, chans = grid.shape
    return grid.reshape(frames, rows // 2, 2, cols // 2, 2, chans).sum(axis=(2, 4))


def scale_back(pooled, preact, norm_gain):
    scaled = norm_gain * preact.astype(jnp.float32)
    sigmoid_val = jax.nn.sigmoid(scaled)
    return (pooled * norm_gain * sigmoid_val * (1.0 + scaled * (1.0 - sigmoid_val))).astype(jnp.bfloat16)


def head_backward(operands):
    query_h, key_h, value_h, grad_h = operands
    score_factor = HEAD_DIM ** -0.5
    scores = score_factor * jnp.dot(query_h, key_h.T, preferred_element_type=jnp.float32)
    peak = jnp.max(scores, axis=-1, keepdims=True)
    expd = jnp.exp(scores - peak)
    probs = expd / jnp.sum(expd, axis=-1, keepdims=True)
    probs_low = probs.astype(jnp.bfloat16)
    attended = jnp.dot(probs_low, value_h, preferred_element_type=jnp.float32)
    row_dot = jnp.sum(grad_h.astype(jnp.float32) * attended, axis=-1)
    grad_probs = jnp.dot(grad_h, value_h.T, preferred_element_type=jnp.float32)
    grad_low = (probs * (grad_probs - row_dot[:, None])).astype(jnp.bfloat16)
    grad_query = score_factor * jnp.dot(grad_low, key_h, preferred_element_type=jnp.float32)
    lower_tiles = grad_low.reshape(N_TX, TOK_DEV, TOKENS).astype(jnp.float32)
    probability_tiles = probs_low.reshape(N_TX, TOK_DEV, TOKENS).astype(jnp.float32)
    query_tiles = query_h.reshape(N_TX, TOK_DEV, HEAD_DIM).astype(jnp.float32)
    gradient_tiles_stacked = grad_h.reshape(N_TX, TOK_DEV, HEAD_DIM).astype(jnp.float32)
    key_products = score_factor * jnp.einsum('tne,tnm->tem', lower_tiles, query_tiles)
    value_products = jnp.einsum('tne,tnm->tem', probability_tiles, gradient_tiles_stacked)
    key_products = lax.optimization_barrier(key_products.astype(jnp.bfloat16))
    value_products = lax.optimization_barrier(value_products.astype(jnp.bfloat16))
    grad_key = jnp.sum(key_products.astype(jnp.float32), axis=0)
    grad_value = jnp.sum(value_products.astype(jnp.float32), axis=0)
    return grad_query, grad_key, grad_value


def split_heads(matrix):
    return matrix.reshape(TOKENS, HEADS, HEAD_DIM).transpose(1, 0, 2)


def join_heads(stacked):
    return stacked.transpose(1, 0, 2).reshape(TOKENS, HEADS * HEAD_DIM)


def reference(out_grad, preact, norm_gain, mid_weight, up_weight, patch_weight, query_proj, key_proj, value_proj, qkv_weight):
    padded = jnp.pad(out_grad, ((0, 0), (1, 1), (1, 1), (0, 0)))
    up_grad = transpose_conv(padded, up_weight)
    pooled = pool_pairs(up_grad)
    mid_grad = scale_back(pooled, preact, norm_gain)
    mid_padded = jnp.pad(mid_grad, ((0, 0), (1, 1), (1, 1), (0, 0)))
    feature_grad = transpose_conv(mid_padded, mid_weight).astype(jnp.bfloat16)
    tiled = feature_grad.reshape(FRAMES, N_TY, ROWS_DEV // 2, 2, N_TX, COLS_DEV // 2, 2, MID_CH)
    patches = tiled.transpose(4, 1, 2, 5, 0, 3, 6, 7).reshape(TOKENS, 4 * FRAMES * MID_CH)
    attn_grad = jnp.dot(patches, patch_weight, preferred_element_type=jnp.float32).astype(jnp.bfloat16)
    operands = (split_heads(query_proj), split_heads(key_proj), split_heads(value_proj), split_heads(attn_grad))
    grad_query, grad_key, grad_value = lax.map(head_backward, operands)
    qkv_grad = jnp.stack([join_heads(grad_query), join_heads(grad_key), join_heads(grad_value)], axis=1).astype(jnp.bfloat16)
    group_cols = HEADS * HEAD_DIM // N_TY
    summed = jnp.zeros((TOKENS, WIDTH), jnp.float32)
    for group in range(N_TY):
        grad_cols = qkv_grad[:, :, group * group_cols:(group + 1) * group_cols].reshape(TOKENS, 3 * group_cols)
        weight_cols = qkv_weight[:, :, group * group_cols:(group + 1) * group_cols].reshape(WIDTH, 3 * group_cols)
        head_part = jnp.dot(grad_cols, weight_cols.T, preferred_element_type=jnp.float32)
        head_part = lax.optimization_barrier(head_part.astype(jnp.bfloat16))
        summed = summed + head_part.astype(jnp.float32)
    latent_grad = summed.astype(jnp.bfloat16)
    return feature_grad, latent_grad
```

```python
import jax
import jax.numpy as jnp
from jax import lax
from jax.sharding import Mesh
from jax.sharding import PartitionSpec as P

HEAD_DIM = 128


def padded(cells, sides, width):
    for axis, dim in sides:
        count = lax.axis_size(axis)
        ends = count - 1
        head = lax.slice_in_dim(cells, 0, width, axis=dim)
        tail = lax.slice_in_dim(cells, cells.shape[dim] - width, cells.shape[dim], axis=dim)
        cells = jnp.concatenate(
            [
                lax.ppermute(tail, axis, [(i, (i + 1) % count) for i in range(ends)]),
                cells,
                lax.ppermute(head, axis, [((i + 1) % count, i) for i in range(ends)]),
            ],
            axis=dim,
        )
    return cells


def conv(cells, weight, stride):
    return lax.conv_general_dilated(
        cells,
        lax.rev(weight, (0, 1)),
        (stride, stride),
        "VALID",
        dimension_numbers=("NHWC", "HWOI", "NHWC"),
        preferred_element_type=jnp.float32,
    )


def causal(cells, weight, stride):
    own = conv(cells, weight[2], stride)
    later = conv(cells[1:], weight[1], stride)
    return own + jnp.pad(later, ((0, 1), (0, 0), (0, 0), (0, 0)))


def scale_back(pooled, preact, norm_gain):
    scaled = norm_gain * preact.astype(jnp.float32)
    sigmoid_val = jax.nn.sigmoid(scaled)
    return (pooled * norm_gain * sigmoid_val * (1.0 + scaled * (1.0 - sigmoid_val))).astype(
        jnp.bfloat16
    )


def body(
    out_grad,
    preact,
    norm_gain,
    mid_weight,
    up_weight,
    patch_weight,
    query_proj,
    key_proj,
    value_proj,
    qkv_weight,
):
    bf = jnp.bfloat16
    f32 = jnp.float32
    w_all = lax.all_gather(qkv_weight, "m", axis=0, tiled=True)
    key_all = lax.all_gather(key_proj, "y", axis=0, tiled=True)
    value_all = lax.all_gather(value_proj, "y", axis=0, tiled=True)
    query_all = lax.all_gather(query_proj, "m", axis=0, tiled=True)
    fine = padded(out_grad, (("ty", 1), (("y", "m"), 2)), 1).astype(f32)
    fine = fine[:, :-1] + fine[:, 1:]
    fine = (fine[:, :, :-1] + fine[:, :, 1:]).astype(bf)
    pooled = causal(fine, up_weight, 2)
    mid_grad = scale_back(pooled, preact, norm_gain)
    mid_pad = padded(mid_grad, (("ty", 1), (("y", "m"), 2)), 1)
    feature_grad = causal(mid_pad, mid_weight, 1).astype(bf)
    frame_count, tile_rows, tile_cols, channels = feature_grad.shape
    patches = feature_grad.reshape(frame_count, tile_rows // 2, 2, tile_cols // 2, 2, channels)
    patches = patches.transpose(1, 3, 0, 2, 4, 5).reshape(
        tile_rows // 2 * (tile_cols // 2), frame_count * 4 * channels
    )
    grad_out = jnp.dot(
        lax.all_gather(patches, "ty", axis=0, tiled=True),
        patch_weight,
        preferred_element_type=f32,
    ).astype(bf)
    tok_count, head_cols = query_proj.shape
    heads = head_cols // HEAD_DIM
    factor = HEAD_DIM ** (-0.5)

    def split(rows):
        return rows.reshape(-1, heads, HEAD_DIM)

    def dots(spec, one, two):
        return jnp.einsum(spec, one, two, preferred_element_type=f32)

    query_h, key_h, value_h = split(query_all), split(key_all), split(value_all)
    scores = factor * dots("qhd,khd->hqk", query_h, key_h)
    peak = lax.pmax(jnp.max(scores, axis=-1, keepdims=True), "m")
    expd = jnp.exp(scores - peak)
    totals = lax.psum(jnp.sum(expd, axis=-1, keepdims=True), "m")
    probs = expd / totals
    probs_low = probs.astype(bf)
    grad_h = split(lax.all_gather(grad_out, "m", axis=0, tiled=True))
    grad_probs = dots("qhd,khd->hqk", grad_h, value_h)
    row_dot = lax.psum(jnp.sum(probs * grad_probs, axis=-1, keepdims=True), "m")
    grad_low = (probs * (grad_probs - row_dot)).astype(bf)
    grad_query = factor * dots("hqk,khd->qhd", grad_low, key_h)
    grad_key = factor * dots("hqk,qhd->khd", grad_low, query_h)
    grad_value = dots("hqk,qhd->khd", probs_low, grad_h)

    def scatter(rows, axis):
        rows = rows.reshape(-1, head_cols).astype(bf)
        return lax.psum_scatter(rows, axis, scatter_dimension=0, tiled=True)

    qkv_grad = jnp.stack(
        [scatter(grad_query, "m"), scatter(grad_key, "y"), scatter(grad_value, "y")], axis=1
    )
    head_part = lax.dot_general(
        lax.all_gather(qkv_grad, "y", axis=0, tiled=True),
        w_all,
        (((1, 2), (1, 2)), ((), ())),
        preferred_element_type=f32,
    )
    part = lax.psum_scatter(head_part.astype(bf), "ty", scatter_dimension=0, tiled=True)
    count = lax.axis_size("ty")
    latent_grad = lax.ppermute(
        part,
        ("ty", "y"),
        [(i * count + j, j * count + i) for i in range(count) for j in range(count)],
    )
    return (feature_grad, latent_grad)


def solution(mesh):
    rows, cols = mesh.devices.shape
    split = Mesh(mesh.devices.reshape(rows, rows, cols // rows), ("ty", "y", "m"))
    tx = ("y", "m")
    placed = (
        P(None, "ty", tx, None),
        P(None, "ty", tx, None),
        P(),
        P(),
        P(),
        P(None, "ty"),
        P(tx, "ty"),
        P(tx, "ty"),
        P(tx, "ty"),
        P(tx, None, "ty"),
    )
    return jax.shard_map(
        body,
        mesh=split,
        in_specs=placed,
        out_specs=(P(None, "ty", tx, None), P(tx, "ty")),
        check_vma=False,
    )
```

```python
import jax
import jax.numpy as jnp
from jax import lax
from jax.experimental import pallas as pl
from jax.experimental.pallas import tpu as pltpu
from jax.sharding import Mesh
from jax.sharding import PartitionSpec as P

HEAD_DIM = 128


BF = jnp.bfloat16
F32 = jnp.float32
MESH = pl.DeviceIdType.MESH
NT = (((1,), (1,)), ((), ()))
TN = (((0,), (0,)), ((), ()))
TY, NY, NM = 4, 4, 8
HEADS, TOK, COLS = 5, 128, 640
QUERIES, KEYS = NM * TOK, NY * TOK
CHUNK = 256
QC = QUERIES // CHUNK
ROWS_W = 160
OUT = NM * ROWS_W
PATCH = 3072
FACTOR = HEAD_DIM ** (-0.5)
LOG2E = 1.4426950408889634


def padded(cells, sides, width):
    for axis, dim in sides:
        count = lax.axis_size(axis)
        ends = count - 1
        head = lax.slice_in_dim(cells, 0, width, axis=dim)
        tail = lax.slice_in_dim(cells, cells.shape[dim] - width, cells.shape[dim], axis=dim)
        cells = jnp.concatenate(
            [
                lax.ppermute(tail, axis, [(i, (i + 1) % count) for i in range(ends)]),
                cells,
                lax.ppermute(head, axis, [((i + 1) % count, i) for i in range(ends)]),
            ],
            axis=dim,
        )
    return cells


def conv(cells, weight, stride):
    return lax.conv_general_dilated(
        cells,
        lax.rev(weight, (0, 1)),
        (stride, stride),
        "VALID",
        dimension_numbers=("NHWC", "HWOI", "NHWC"),
        preferred_element_type=jnp.float32,
    )


def causal(cells, weight, stride):
    own = conv(cells, weight[2], stride)
    later = conv(cells[1:], weight[1], stride)
    return own + jnp.pad(later, ((0, 1), (0, 0), (0, 0), (0, 0)))


def scale_back(pooled, preact, norm_gain):
    scaled = norm_gain * preact.astype(jnp.float32)
    sigmoid_val = jax.nn.sigmoid(scaled)
    return (pooled * norm_gain * sigmoid_val * (1.0 + scaled * (1.0 - sigmoid_val))).astype(
        jnp.bfloat16
    )


def mm(one, two, dims=(((1,), (0,)), ((), ()))):
    return lax.dot_general(one, two, dims, preferred_element_type=F32)


def attend_kernel(
    patches, patch_w, query, key, value, weight, out,
    p_all, pw, q_all, k_all, v_all, g_all, w_all, probs, gp, stat_s, stat_r, dot_s, dot_r,
    dq_s, dq_r, dk_s, dk_r, dv_s, dv_r, a_all, part, red,
    sem_p, sem_q, sem_k, sem_v, sem_w, sem_g, sem_st, sem_rd, sem_dq, sem_dk, sem_dv, sem_a, sem_o, sem_l,
):
    c, y, m = lax.axis_index("ty"), lax.axis_index("y"), lax.axis_index("m")

    def in_c(step):
        return (lax.rem(c + step, TY), y, m)

    def in_y(step):
        return (c, lax.rem(y + step, NY), m)

    def in_m(step):
        return (c, y, lax.rem(m + step, NM))

    def rows(index, size=TOK):
        return pl.ds(pl.multiple_of(index * size, size), size)

    def cols(h):
        return pl.ds(pl.multiple_of(h * HEAD_DIM, HEAD_DIM), HEAD_DIM)

    def push(src, dst, sems, index, target):
        return pltpu.make_async_remote_copy(
            src_ref=src, dst_ref=dst, send_sem=sems.at[0, index], recv_sem=sems.at[1, index],
            device_id=target, device_id_type=MESH,
        )

    barrier = pltpu.get_barrier_semaphore()
    for dc in range(TY):
        for dy in range(NY):
            if dc or dy:
                pl.semaphore_signal(
                    barrier, inc=1, device_id_type=MESH,
                    device_id=(lax.rem(c + dc, TY), lax.rem(y + dy, NY), m),
                )
    for dm in range(1, NM):
        pl.semaphore_signal(barrier, inc=1, device_id=in_m(dm), device_id_type=MESH)

    local = [
        pltpu.make_async_copy(patches, p_all.at[rows(c, 32)], sem_l.at[0]),
        pltpu.make_async_copy(query, q_all.at[rows(m)], sem_l.at[1]),
        pltpu.make_async_copy(key, k_all.at[rows(y)], sem_l.at[2]),
        pltpu.make_async_copy(value, v_all.at[rows(y)], sem_l.at[3]),
        pltpu.make_async_copy(weight, w_all.at[:, rows(m, ROWS_W)], sem_l.at[4]),
        pltpu.make_async_copy(patch_w, pw, sem_l.at[5]),
    ]
    for copy in local:
        copy.start()
    pl.semaphore_wait(barrier, TY * NY - 1 + NM - 1)

    to_p = [push(patches, p_all.at[rows(c, 32)], sem_p, d, in_c(d)) for d in range(1, TY)]
    to_k = [push(key, k_all.at[rows(y)], sem_k, d, in_y(d)) for d in range(1, NY)]
    to_q = [push(query, q_all.at[rows(m)], sem_q, d, in_m(d)) for d in range(1, NM)]
    to_v = [push(value, v_all.at[rows(y)], sem_v, d, in_y(d)) for d in range(1, NY)]
    to_w = [push(weight, w_all.at[:, rows(m, ROWS_W)], sem_w, d, in_m(d)) for d in range(1, NM)]
    for copy in to_p + to_k + to_q + to_v + to_w:
        copy.start()

    for copy in local:
        copy.wait()
    for copy in to_p:
        copy.wait_recv()
    g_all[rows(m), :] = mm(p_all[...], pw[...]).astype(BF)
    to_g = [push(g_all.at[rows(m)], g_all.at[rows(m)], sem_g, d, in_m(d)) for d in range(1, NM)]
    for copy in to_g:
        copy.start()

    for copy in to_k + to_q:
        copy.wait_recv()

    def score_step(i, _):
        h, qc = i // QC, lax.rem(i, QC)
        span = rows(qc, CHUNK)
        s = mm(k_all[:, cols(h)], q_all[span, cols(h)], NT) * (FACTOR * LOG2E)
        peak = jnp.max(s, axis=0, keepdims=True)
        e = jnp.exp2(s - peak)
        stat_s[h, :, span] = peak
        stat_s[HEADS + h, :, span] = jnp.sum(e, axis=0, keepdims=True)
        probs[h, :, span] = e.astype(BF)
        return 0

    lax.fori_loop(0, HEADS * QC, score_step, 0)
    to_st = [push(stat_s, stat_r.at[m], sem_st, d, in_m(d)) for d in range(1, NM)]
    for copy in to_st:
        copy.start()
    stat_r[m] = stat_s[...]
    for copy in to_st + to_v + to_g:
        copy.wait_recv()

    def grad_step(i, _):
        h, qc = i // QC, lax.rem(i, QC)
        span = rows(qc, CHUNK)
        peaks = [stat_r[j, h, :, span] for j in range(NM)]
        top = peaks[0]
        for j in range(1, NM):
            top = jnp.maximum(top, peaks[j])
        total = jnp.zeros_like(top)
        for j in range(NM):
            total = total + stat_r[j, HEADS + h, :, span] * jnp.exp2(peaks[j] - top)
        share = jnp.exp2(stat_s[h, :, span] - top) / total
        p = probs[h, :, span].astype(F32) * share
        g = mm(v_all[:, cols(h)], g_all[span, cols(h)], NT)
        dot_s[h, :, span] = jnp.sum(p * g, axis=0, keepdims=True)
        probs[h, :, span] = p.astype(BF)
        gp[h, :, span] = g.astype(BF)
        return 0

    lax.fori_loop(0, HEADS * QC, grad_step, 0)
    to_rd = [push(dot_s, dot_r.at[m], sem_rd, d, in_m(d)) for d in range(1, NM)]
    for copy in to_rd:
        copy.start()
    dot_r[m] = dot_s[...]

    def dv_copies(h):
        return [
            push(dv_s.at[rows(lax.rem(y + d, NY)), cols(h)], dv_r.at[rows(y), cols(h)], sem_dv, h * NY + d, in_y(d))
            for d in range(1, NY)
        ]

    def dk_copies(h):
        return [
            push(dk_s.at[rows(lax.rem(y + d, NY)), cols(h)], dk_r.at[rows(y), cols(h)], sem_dk, h * NY + d, in_y(d))
            for d in range(1, NY)
        ]

    def dq_copies(h):
        return [
            push(dq_s.at[rows(lax.rem(m + d, NM)), cols(h)], dq_r.at[rows(m), cols(h)], sem_dq, h * NM + d, in_m(d))
            for d in range(1, NM)
        ]

    def a_copies(h):
        return [
            push(a_all.at[:, rows(y), cols(h)], a_all.at[:, rows(y), cols(h)], sem_a, h * NY + d, in_y(d))
            for d in range(1, NY)
        ]

    def value_step(h, _):
        dv_s[:, cols(h)] = mm(probs[h], g_all[:, cols(h)]).astype(BF)
        for copy in dv_copies(h):
            copy.start()
        return 0

    lax.fori_loop(0, HEADS, value_step, 0)
    for copy in to_rd:
        copy.wait_recv()

    def key_step(h, _):
        for qc in range(QC):
            span = pl.ds(qc * CHUNK, CHUNK)
            dot = dot_r[0, h, :, span]
            for j in range(1, NM):
                dot = dot + dot_r[j, h, :, span]
            ds = (probs[h, :, span].astype(F32) * (gp[h, :, span].astype(F32) - dot)).astype(BF)
            gp[h, :, span] = ds
            dq_s[span, cols(h)] = (FACTOR * mm(ds, k_all[:, cols(h)], TN)).astype(BF)
        for copy in dq_copies(h):
            copy.start()
        dk_s[:, cols(h)] = (FACTOR * mm(gp[h], q_all[:, cols(h)])).astype(BF)
        for copy in dk_copies(h):
            copy.start()
        return 0

    lax.fori_loop(0, HEADS, key_step, 0)

    def sum_step(h, _):
        for copy in dq_copies(h) + dk_copies(h) + dv_copies(h):
            copy.wait_recv()
        dq = dq_s[rows(m), cols(h)].astype(F32)
        for d in range(1, NM):
            dq = dq + dq_r[rows(lax.rem(m + d, NM)), cols(h)].astype(F32)
        dk = dk_s[rows(y), cols(h)].astype(F32)
        dv = dv_s[rows(y), cols(h)].astype(F32)
        for d in range(1, NY):
            other = rows(lax.rem(y + d, NY))
            dk = dk + dk_r[other, cols(h)].astype(F32)
            dv = dv + dv_r[other, cols(h)].astype(F32)
        a_all[0, rows(y), cols(h)] = dq.astype(BF)
        a_all[1, rows(y), cols(h)] = dk.astype(BF)
        a_all[2, rows(y), cols(h)] = dv.astype(BF)
        for copy in a_copies(h):
            copy.start()
        return 0

    lax.fori_loop(0, HEADS, sum_step, 0)
    for copy in to_w:
        copy.wait_recv()

    def arrive(h, _):
        for copy in a_copies(h):
            copy.wait_recv()
        return 0

    lax.fori_loop(0, HEADS, arrive, 0)

    def out_copy(n, d):
        span = pl.ds(pl.multiple_of(n * CHUNK, CHUNK), CHUNK)
        to = lax.rem(y + d, NY)
        return pltpu.make_async_remote_copy(
            src_ref=part.at[rows(to), span], dst_ref=red.at[rows(c), span],
            send_sem=sem_o.at[0, n * NY + d], recv_sem=sem_o.at[1, n * NY + c],
            device_id=(y, to, m), device_id_type=MESH,
        )

    def project(n, _):
        span = pl.ds(pl.multiple_of(n * CHUNK, CHUNK), CHUNK)
        total = mm(a_all[0], w_all[0, span, :], NT)
        total = total + mm(a_all[1], w_all[1, span, :], NT)
        total = total + mm(a_all[2], w_all[2, span, :], NT)
        part[:, span] = total.astype(BF)
        for d in range(1, NY):
            out_copy(n, d).start()

        @pl.when(c == y)
        def _():
            red[rows(c), span] = part[rows(y), span]

        @pl.when(c != y)
        def _():
            out_copy(n, 0).start()

        return 0

    lax.fori_loop(0, OUT // CHUNK, project, 0)

    step = lax.rem(y - c + NY, NY)

    def finish(n, _):
        span = pl.ds(pl.multiple_of(n * CHUNK, CHUNK), CHUNK)
        for other in range(TY):
            @pl.when((c != y) | (c != other))
            def _():
                pltpu.make_async_remote_copy(
                    src_ref=part.at[rows(0), span], dst_ref=red.at[rows(other), span],
                    send_sem=sem_o.at[0, n * NY], recv_sem=sem_o.at[1, n * NY + other],
                    device_id=in_y(1), device_id_type=MESH,
                ).wait_recv()
        total = red[rows(0), span].astype(F32)
        for other in range(1, TY):
            total = total + red[rows(other), span].astype(F32)
        out[:, span] = total.astype(BF)
        return 0

    lax.fori_loop(0, OUT // CHUNK, finish, 0)

    for copy in to_p + to_k + to_q + to_v + to_w + to_g + to_st + to_rd:
        copy.wait_send()

    def sent(h, _):
        for copy in dv_copies(h) + dk_copies(h) + dq_copies(h) + a_copies(h):
            copy.wait_send()
        return 0

    lax.fori_loop(0, HEADS, sent, 0)

    def out_sent(n, _):
        for d in range(1, NY):
            out_copy(n, d).wait_send()

        @pl.when(c != y)
        def _():
            out_copy(n, 0).wait_send()

        return 0

    lax.fori_loop(0, OUT // CHUNK, out_sent, 0)


def body(
    out_grad,
    preact,
    norm_gain,
    mid_weight,
    up_weight,
    patch_weight,
    query_proj,
    key_proj,
    value_proj,
    qkv_weight,
):
    fine = padded(out_grad, (("ty", 1), (("y", "m"), 2)), 1).astype(F32)
    fine = fine[:, :-1] + fine[:, 1:]
    fine = (fine[:, :, :-1] + fine[:, :, 1:]).astype(BF)
    pooled = causal(fine, up_weight, 2)
    mid_grad = scale_back(pooled, preact, norm_gain)
    mid_pad = padded(mid_grad, (("ty", 1), (("y", "m"), 2)), 1)
    feature_grad = causal(mid_pad, mid_weight, 1).astype(BF)
    frame_count, tile_rows, tile_cols, channels = feature_grad.shape
    patches = feature_grad.reshape(frame_count, tile_rows // 2, 2, tile_cols // 2, 2, channels)
    patches = patches.transpose(1, 3, 0, 2, 4, 5).reshape(
        tile_rows // 2 * (tile_cols // 2), frame_count * 4 * channels
    )
    any_space = pl.BlockSpec(memory_space=pl.ANY)

    def sems(count):
        return pltpu.SemaphoreType.DMA((2, count))

    latent_grad = pl.pallas_call(
        attend_kernel,
        out_shape=jax.ShapeDtypeStruct((TOK, OUT), BF),
        in_specs=[any_space] * 6,
        out_specs=pl.BlockSpec(memory_space=pltpu.VMEM),
        scratch_shapes=[
            pltpu.VMEM((TOK, PATCH), BF),
            pltpu.VMEM((PATCH, COLS), BF),
            pltpu.VMEM((QUERIES, COLS), BF),
            pltpu.VMEM((KEYS, COLS), BF),
            pltpu.VMEM((KEYS, COLS), BF),
            pltpu.VMEM((QUERIES, COLS), BF),
            pltpu.VMEM((3, OUT, COLS), BF),
            pltpu.VMEM((HEADS, KEYS, QUERIES), BF),
            pltpu.VMEM((HEADS, KEYS, QUERIES), BF),
            pltpu.VMEM((2 * HEADS, 1, QUERIES), F32),
            pltpu.VMEM((NM, 2 * HEADS, 1, QUERIES), F32),
            pltpu.VMEM((HEADS, 1, QUERIES), F32),
            pltpu.VMEM((NM, HEADS, 1, QUERIES), F32),
            pltpu.VMEM((QUERIES, COLS), BF),
            pltpu.VMEM((QUERIES, COLS), BF),
            pltpu.VMEM((KEYS, COLS), BF),
            pltpu.VMEM((KEYS, COLS), BF),
            pltpu.VMEM((KEYS, COLS), BF),
            pltpu.VMEM((KEYS, COLS), BF),
            pltpu.VMEM((3, KEYS, COLS), BF),
            pltpu.VMEM((KEYS, OUT), BF),
            pltpu.VMEM((KEYS, OUT), BF),
            sems(TY),
            sems(NM),
            sems(NY),
            sems(NY),
            sems(NM),
            sems(NM),
            sems(NM),
            sems(NM),
            sems(HEADS * NM),
            sems(HEADS * NY),
            sems(HEADS * NY),
            sems(HEADS * NY),
            sems(OUT // CHUNK * NY),
            pltpu.SemaphoreType.DMA((6,)),
        ],
        compiler_params=pltpu.CompilerParams(
            collective_id=0, has_side_effects=True, vmem_limit_bytes=56 * 1024 * 1024
        ),
        name="attend",
    )(patches, patch_weight, query_proj, key_proj, value_proj, qkv_weight.transpose(1, 0, 2))
    return (feature_grad, latent_grad)


def solution(mesh):
    rows, cols = mesh.devices.shape
    split = Mesh(mesh.devices.reshape(rows, rows, cols // rows), ("ty", "y", "m"))
    tx = ("y", "m")
    placed = (
        P(None, "ty", tx, None),
        P(None, "ty", tx, None),
        P(),
        P(),
        P(),
        P(None, "ty"),
        P(tx, "ty"),
        P(tx, "ty"),
        P(tx, "ty"),
        P(tx, None, "ty"),
    )
    return jax.shard_map(
        body,
        mesh=split,
        in_specs=placed,
        out_specs=(P(None, "ty", tx, None), P(tx, "ty")),
        check_vma=False,
    )
```

```python
import jax
import jax.numpy as jnp
from jax import lax
from jax.experimental import pallas as pl
from jax.experimental.pallas import tpu as pltpu
from jax.sharding import Mesh
from jax.sharding import PartitionSpec as P

HEAD_DIM = 128

BF = jnp.bfloat16
F32 = jnp.float32
MESH = pl.DeviceIdType.MESH
NN = (((1,), (0,)), ((), ()))
NT = (((1,), (1,)), ((), ()))
TN = (((0,), (0,)), ((), ()))
AXES = ("zl", "core", "y", "x", "zh")
SIZES = (2, 2, 4, 4, 2)
NX, NY, NZ, TY = 4, 4, 2, 4
NK = NX * NZ
HEADS, TOK, COLS = 5, 128, 640
FULL = NX * NY * TOK
LAST = NY * TOK
QUERIES = FULL + LAST
KEYS = NK * TOK
CHUNK = 256
FULL_CHUNKS = FULL // CHUNK
CHUNKS = QUERIES // CHUNK
ROWS_W = 160
CUT_W = 64
OUT = NK * ROWS_W
HALF = OUT // 2
PIECES = ((0, 256), (256, 256), (512, 128))
PATCH = 3072
FACTOR = HEAD_DIM ** (-0.5)
LOG2E = 1.4426950408889634


def mm(one, two, dims=NN):
    return lax.dot_general(one, two, dims, preferred_element_type=F32)


def wide(tile):
    return tile.astype(F32)


def attend_kernel(
    patches, patch_w, query, key, value, weight, out,
    p_all, pw, q_all, k_all, v_all, g_own, g_all, w_all, probs, gp, stat_s, stat_r, dot_s, dot_r,
    dq_s, dq_r, dl_r, dk_s, dk_r, dv_s, dv_r, a_all, part, pair, red,
    sem_p, sem_q, sem_k, sem_v, sem_w, sem_g, sem_st, sem_rd, sem_dq, sem_dk, sem_dv, sem_a, sem_c, sem_o, sem_l,
):
    zl, core, y, x, zh = [lax.axis_index(name) for name in AXES]
    c = zl * 2 + core

    def at(dty=0, dy=0, dx=0, dz=0):
        ty = lax.rem(c + dty, TY)
        return (ty // 2, lax.rem(ty, 2), lax.rem(y + dy, NY), lax.rem(x + dx, NX), lax.rem(zh + dz, NZ))

    partner = (zl, 1 - core, y, x, zh)

    def rows(index, size=TOK, base=0):
        return pl.ds(pl.multiple_of(index * size + base, 32), size)

    def cols(h):
        return pl.ds(pl.multiple_of(h * HEAD_DIM, HEAD_DIM), HEAD_DIM)

    def push(src, dst, sems, index, target, arrives=None):
        return pltpu.make_async_remote_copy(
            src_ref=src, dst_ref=dst, send_sem=sems.at[0, index],
            recv_sem=sems.at[1, index if arrives is None else arrives],
            device_id=target, device_id_type=MESH,
        )

    def start(copies):
        for copy in copies:
            copy.start()

    def arrived(copies):
        for copy in copies:
            copy.wait_recv()

    greet = [at(dty=a, dy=b) for a in range(TY) for b in range(NY) if a or b]
    greet += [at(dy=a, dx=b) for a in range(NY) for b in range(1, NX)]
    greet += [at(dx=a, dz=1) for a in range(NX)]
    barrier = pltpu.get_barrier_semaphore()
    for other in greet:
        pl.semaphore_signal(barrier, inc=1, device_id=other, device_id_type=MESH)

    plane = y * NX + x
    line = x * NZ + zh
    local = [
        pltpu.make_async_copy(patches, p_all.at[rows(c, 32)], sem_l.at[0]),
        pltpu.make_async_copy(patch_w, pw, sem_l.at[1]),
        pltpu.make_async_copy(query.at[:, cols(x)], q_all.at[rows(plane)], sem_l.at[2]),
        pltpu.make_async_copy(query.at[:, cols(NX)], q_all.at[rows(y, base=FULL)], sem_l.at[3]),
        pltpu.make_async_copy(key.at[:, cols(x)], k_all.at[rows(line)], sem_l.at[4]),
        pltpu.make_async_copy(key.at[:, cols(NX)], k_all.at[rows(line, base=KEYS)], sem_l.at[5]),
        pltpu.make_async_copy(value.at[:, cols(x)], v_all.at[rows(line)], sem_l.at[6]),
        pltpu.make_async_copy(value.at[:, cols(NX)], v_all.at[rows(line, base=KEYS)], sem_l.at[7]),
        pltpu.make_async_copy(weight, w_all.at[:, rows(line, ROWS_W)], sem_l.at[8]),
    ]
    start(local)
    pl.semaphore_wait(barrier, len(greet))

    def to_queries(src, dst, sems):
        copies = []
        for dy in range(NY):
            for dx in range(NX):
                if dy or dx:
                    head = cols(lax.rem(x + dx, NX))
                    copies.append(push(src.at[:, head], dst.at[rows(plane)], sems, dy * NX + dx, at(dy=dy, dx=dx)))
            if dy:
                copies.append(push(src.at[:, cols(NX)], dst.at[rows(y, base=FULL)], sems, NY * NX + dy, at(dy=dy)))
        return copies

    def to_keys(src, dst, sems):
        copies = []
        for dz in range(NZ):
            for dx in range(NX):
                if dz or dx:
                    head = cols(lax.rem(x + dx, NX))
                    target = at(dx=dx, dz=dz)
                    slot = 2 * (dx * NZ + dz)
                    copies.append(push(src.at[:, head], dst.at[rows(line)], sems, slot, target))
                    copies.append(push(src.at[:, cols(NX)], dst.at[rows(line, base=KEYS)], sems, slot + 1, target))
        return copies

    to_p = [push(patches, p_all.at[rows(c, 32)], sem_p, d, at(dty=d)) for d in range(1, TY)]
    to_k = to_keys(key, k_all, sem_k)
    to_q = to_queries(query, q_all, sem_q)
    to_v = to_keys(value, v_all, sem_v)
    mine = w_all.at[:, rows(line, ROWS_W)]
    to_w = [push(weight, mine, sem_w, d, at(dx=d)) for d in range(1, NX)]
    to_w.append(push(weight, mine, sem_w, 0, at(dz=1)))
    start(to_p + to_k + to_q + to_v + to_w)
    beside = w_all.at[:, pl.ds(pl.multiple_of((x * NZ + 1 - zh) * ROWS_W, 32), CUT_W)]
    on_x = [push(beside, beside, sem_w, NX + d, at(dx=d)) for d in range(1, NX)]
    on_z = []
    for d in range(1, NX):
        first = lax.rem(x - d + NX, NX) * NZ + zh
        below = w_all.at[:, pl.ds(pl.multiple_of(first * ROWS_W + CUT_W, 32), ROWS_W - CUT_W)]
        on_z.append(push(below, below, sem_w, 2 * NX + d, at(dz=1)))

    for copy in local:
        copy.wait()
    arrived(to_p)
    g_own[...] = mm(p_all[...], pw[...]).astype(BF)
    to_g = to_queries(g_own, g_all, sem_g)
    start(to_g)
    g_all[rows(plane), :] = g_own[:, cols(x)]
    g_all[rows(y, base=FULL), :] = g_own[:, cols(NX)]

    arrived(to_k + to_q)

    def spans(i):
        return rows(i, CHUNK), rows(i // FULL_CHUNKS, KEYS)

    def score_step(i, _):
        span, keys = spans(i)
        s = mm(k_all[keys, :], q_all[span, :], NT) * (FACTOR * LOG2E)
        peak = jnp.max(s, axis=0, keepdims=True)
        e = jnp.exp2(s - peak)
        stat_s[0, :, span] = peak
        stat_s[1, :, span] = jnp.sum(e, axis=0, keepdims=True)
        probs[:, span] = e.astype(BF)
        return 0

    lax.fori_loop(0, CHUNKS, score_step, 0)
    to_st = [push(stat_s, stat_r.at[y], sem_st, d, at(dy=d)) for d in range(1, NY)]
    start(to_st)
    stat_r[y] = stat_s[...]
    arrived(to_st)

    def share_step(i, _):
        span, _ = spans(i)
        top = stat_r[0, 0, :, span]
        for j in range(1, NY):
            top = jnp.maximum(top, stat_r[j, 0, :, span])
        total = jnp.zeros_like(top)
        for j in range(NY):
            total = total + stat_r[j, 1, :, span] * jnp.exp2(stat_r[j, 0, :, span] - top)
        share = jnp.exp2(stat_s[0, :, span] - top) / total
        probs[:, span] = (wide(probs[:, span]) * share).astype(BF)
        return 0

    lax.fori_loop(0, CHUNKS, share_step, 0)
    arrived(to_v + to_g)

    def grad_step(i, _):
        span, keys = spans(i)
        g = mm(v_all[keys, :], g_all[span, :], NT)
        dot_s[:, span] = jnp.sum(wide(probs[:, span]) * g, axis=0, keepdims=True)
        gp[:, span] = g.astype(BF)
        return 0

    lax.fori_loop(0, CHUNKS, grad_step, 0)
    to_rd = [push(dot_s, dot_r.at[y], sem_rd, d, at(dy=d)) for d in range(1, NY)]
    start(to_rd)
    dot_r[y] = dot_s[...]

    def key_copies(d, made, got, sems):
        copies = []
        block = lax.rem(x + d, NX) * NZ
        for dz in range(NZ):
            if d or dz:
                there = block + lax.rem(zh + dz, NZ)
                for k in range(2):
                    copies.append(
                        push(made.at[k, rows(there)], got.at[line, k], sems, 2 * (d * NZ + dz) + k, at(dx=d, dz=dz))
                    )
        return copies

    def key_sums(left, right, made, got, sems, scale):
        for d in (2, 1, 3, 0):
            block = rows(lax.rem(x + d, NX), NZ * TOK)
            made[0, block, :] = (scale * mm(left[block, :FULL], right[:FULL, :])).astype(BF)
            made[1, block, :] = (scale * mm(left[block, FULL:], right[FULL:, :])).astype(BF)
            start(key_copies(d, made, got, sems))
        got[line] = made[:, rows(line), :]

    def all_key_copies(made, got, sems):
        return [copy for d in range(NX) for copy in key_copies(d, made, got, sems)]

    key_sums(probs, g_all, dv_s, dv_r, sem_dv, 1.0)
    to_dv = all_key_copies(dv_s, dv_r, sem_dv)
    arrived(to_rd)
    arrived(to_w)
    start(on_x + on_z)

    def query_copies(d):
        copies = []
        there = lax.rem(y + d, NY)
        for dx in range(NX):
            if d or dx:
                block = rows(there * NX + lax.rem(x + dx, NX))
                copies.append(push(dq_s.at[block], dq_r.at[plane], sem_dq, d * NX + dx, at(dy=d, dx=dx)))
        return copies

    def last_copy(d):
        block = rows(lax.rem(y + d, NY), base=FULL)
        return push(dq_s.at[block], dl_r.at[y], sem_dq, NY * NX + d, at(dy=d))

    def query_step(i, _):
        span, keys = spans(i)
        dot = dot_r[0, :, span]
        for j in range(1, NY):
            dot = dot + dot_r[j, :, span]
        ds = (wide(probs[:, span]) * (wide(gp[:, span]) - dot)).astype(BF)
        gp[:, span] = ds
        dq_s[span, :] = (FACTOR * mm(ds, k_all[keys, :], TN)).astype(BF)
        return 0

    for d in (2, 1, 3, 0):
        first = lax.rem(y + d, NY) * 2
        lax.fori_loop(first, first + 2, query_step, 0)
        start(query_copies(d))
    lax.fori_loop(FULL_CHUNKS, CHUNKS, query_step, 0)
    to_dl = [last_copy(d) for d in range(1, NY)]
    start(to_dl)
    dq_r[plane] = dq_s[rows(plane), :]
    dl_r[y] = dq_s[rows(y, base=FULL), :]
    key_sums(gp, q_all, dk_s, dk_r, sem_dk, FACTOR)
    to_dk = all_key_copies(dk_s, dk_r, sem_dk)
    to_dq = [copy for d in range(NY) for copy in query_copies(d)]

    def key_total(part_index, got):
        for h in range(NX):
            total = wide(got[h * NZ, 0])
            for j in range(1, NZ):
                total = total + wide(got[h * NZ + j, 0])
            a_all[part_index, rows(y), h * HEAD_DIM : (h + 1) * HEAD_DIM] = total.astype(BF)
        total = wide(got[0, 1])
        for j in range(1, NK):
            total = total + wide(got[j, 1])
        a_all[part_index, rows(y), NX * HEAD_DIM :] = total.astype(BF)

    def a_copies(k):
        mine = a_all.at[k, rows(y)]
        return [push(mine, mine, sem_a, k * NY + d, at(dy=d)) for d in range(1, NY)]

    to_a = [a_copies(k) for k in range(3)]
    arrived(to_dv)
    key_total(2, dv_r)
    start(to_a[2])
    arrived(to_dq + to_dl)
    for h in range(NX):
        total = wide(dq_r[h])
        for j in range(1, NY):
            total = total + wide(dq_r[j * NX + h])
        a_all[0, rows(y), h * HEAD_DIM : (h + 1) * HEAD_DIM] = total.astype(BF)
    total = wide(dl_r[0])
    for j in range(1, NY):
        total = total + wide(dl_r[j])
    a_all[0, rows(y), NX * HEAD_DIM :] = total.astype(BF)
    start(to_a[0])
    arrived(to_dk)
    key_total(1, dk_r)
    start(to_a[1])
    arrived(on_x + on_z)
    for k in (2, 0, 1):
        arrived(to_a[k])

    def project(first, size):
        span = pl.ds(pl.multiple_of(first, HEAD_DIM), size)
        total = mm(a_all[0], w_all[0, span, :], NT)
        total = total + mm(a_all[1], w_all[1, span, :], NT)
        return total + mm(a_all[2], w_all[2, span, :], NT)

    to_c = []
    for n, (first, size) in enumerate(PIECES):
        part[:, first : first + size] = project((1 - core) * HALF + first, size).astype(BF)
        span = pl.ds(first, size)
        copy = push(part.at[:, span], pair.at[:, span], sem_c, n, partner)
        copy.start()
        to_c.append(copy)

    def out_copy(n, d):
        first, size = PIECES[n]
        to = lax.rem(y + d, NY)
        span = pl.ds(pl.multiple_of(core * HALF + first, HEAD_DIM), size)
        return push(
            pair.at[rows(to), pl.ds(first, size)], red.at[zl, :, span], sem_o, n * NY + d,
            (y // 2, lax.rem(y, 2), to, x, zh), n * NY + c,
        )

    for n, (first, size) in enumerate(PIECES):
        total = project(core * HALF + first, size)
        to_c[n].wait_recv()
        span = pl.ds(first, size)
        pair[:, span] = (total + wide(pair[:, span])).astype(BF)
        for d in (2, 1, 3):
            out_copy(n, d).start()

        @pl.when(c == y)
        def _():
            red[zl, :, pl.ds(pl.multiple_of(core * HALF + first, HEAD_DIM), size)] = pair[rows(y), span]

        @pl.when(c != y)
        def _():
            out_copy(n, 0).start()

    for n, (first, size) in enumerate(PIECES):
        for other in range(TY):
            @pl.when((c != y) | (c != other))
            def _():
                push(
                    pair.at[rows(0), pl.ds(first, size)], red.at[other // 2, :, pl.ds((other % 2) * HALF + first, size)],
                    sem_o, n * NY, at(dy=1), n * NY + other,
                ).wait_recv()
        for half in range(2):
            span = pl.ds(half * HALF + first, size)
            out[:, span] = (wide(red[0, :, span]) + wide(red[1, :, span])).astype(BF)

    done = to_p + to_k + to_q + to_v + to_w + on_x + on_z + to_g + to_st + to_rd + to_dv + to_dq + to_dl + to_dk
    for copy in done + to_a[0] + to_a[1] + to_a[2] + to_c:
        copy.wait_send()
    for n in range(len(PIECES)):
        for d in range(1, NY):
            out_copy(n, d).wait_send()

        @pl.when(c != y)
        def _():
            out_copy(n, 0).wait_send()


def padded(cells, sides, width):
    for axis, dim in sides:
        count = lax.axis_size(axis)
        ends = count - 1
        head = lax.slice_in_dim(cells, 0, width, axis=dim)
        tail = lax.slice_in_dim(cells, cells.shape[dim] - width, cells.shape[dim], axis=dim)
        cells = jnp.concatenate(
            [
                lax.ppermute(tail, axis, [(i, (i + 1) % count) for i in range(ends)]),
                cells,
                lax.ppermute(head, axis, [((i + 1) % count, i) for i in range(ends)]),
            ],
            axis=dim,
        )
    return cells


def conv(cells, weight, stride):
    return lax.conv_general_dilated(
        cells,
        lax.rev(weight, (0, 1)),
        (stride, stride),
        "VALID",
        dimension_numbers=("NHWC", "HWOI", "NHWC"),
        preferred_element_type=jnp.float32,
    )


def causal(cells, weight, stride):
    own = conv(cells, weight[2], stride)
    later = conv(cells[1:], weight[1], stride)
    return own + jnp.pad(later, ((0, 1), (0, 0), (0, 0), (0, 0)))


def scale_back(pooled, preact, norm_gain):
    scaled = norm_gain * preact.astype(jnp.float32)
    sigmoid_val = jax.nn.sigmoid(scaled)
    return (pooled * norm_gain * sigmoid_val * (1.0 + scaled * (1.0 - sigmoid_val))).astype(
        jnp.bfloat16
    )


def body(
    out_grad,
    preact,
    norm_gain,
    mid_weight,
    up_weight,
    patch_weight,
    query_proj,
    key_proj,
    value_proj,
    qkv_weight,
):
    fine = padded(out_grad, ((("zl", "core"), 1), (("y", "x", "zh"), 2)), 1).astype(F32)
    fine = fine[:, :-1] + fine[:, 1:]
    fine = (fine[:, :, :-1] + fine[:, :, 1:]).astype(BF)
    pooled = causal(fine, up_weight, 2)
    mid_grad = scale_back(pooled, preact, norm_gain)
    mid_pad = padded(mid_grad, ((("zl", "core"), 1), (("y", "x", "zh"), 2)), 1)
    feature_grad = causal(mid_pad, mid_weight, 1).astype(BF)
    frame_count, tile_rows, tile_cols, channels = feature_grad.shape
    patches = feature_grad.reshape(frame_count, tile_rows // 2, 2, tile_cols // 2, 2, channels)
    patches = patches.transpose(1, 3, 0, 2, 4, 5).reshape(
        tile_rows // 2 * (tile_cols // 2), frame_count * 4 * channels
    )
    any_space = pl.BlockSpec(memory_space=pl.ANY)

    def sems(count):
        return pltpu.SemaphoreType.DMA((2, count))

    latent_grad = pl.pallas_call(
        attend_kernel,
        out_shape=jax.ShapeDtypeStruct((TOK, OUT), BF),
        in_specs=[any_space] * 6,
        out_specs=pl.BlockSpec(memory_space=pltpu.VMEM),
        scratch_shapes=[
            pltpu.VMEM((TOK, PATCH), BF),
            pltpu.VMEM((PATCH, COLS), BF),
            pltpu.VMEM((QUERIES, HEAD_DIM), BF),
            pltpu.VMEM((2 * KEYS, HEAD_DIM), BF),
            pltpu.VMEM((2 * KEYS, HEAD_DIM), BF),
            pltpu.VMEM((TOK, COLS), BF),
            pltpu.VMEM((QUERIES, HEAD_DIM), BF),
            pltpu.VMEM((3, OUT, COLS), BF),
            pltpu.VMEM((KEYS, QUERIES), BF),
            pltpu.VMEM((KEYS, QUERIES), BF),
            pltpu.VMEM((2, 1, QUERIES), F32),
            pltpu.VMEM((NY, 2, 1, QUERIES), F32),
            pltpu.VMEM((1, QUERIES), F32),
            pltpu.VMEM((NY, 1, QUERIES), F32),
            pltpu.VMEM((QUERIES, HEAD_DIM), BF),
            pltpu.VMEM((NY * NX, TOK, HEAD_DIM), BF),
            pltpu.VMEM((NY, TOK, HEAD_DIM), BF),
            pltpu.VMEM((2, KEYS, HEAD_DIM), BF),
            pltpu.VMEM((NK, 2, TOK, HEAD_DIM), BF),
            pltpu.VMEM((2, KEYS, HEAD_DIM), BF),
            pltpu.VMEM((NK, 2, TOK, HEAD_DIM), BF),
            pltpu.VMEM((3, LAST, COLS), BF),
            pltpu.VMEM((LAST, HALF), BF),
            pltpu.VMEM((LAST, HALF), BF),
            pltpu.VMEM((2, TOK, OUT), BF),
            sems(TY),
            sems(NY * NX + NY),
            sems(2 * NK),
            sems(2 * NK),
            sems(3 * NX),
            sems(NY * NX + NY),
            sems(NY),
            sems(NY),
            sems(NY * NX + NY),
            sems(2 * NK),
            sems(2 * NK),
            sems(3 * NY),
            sems(len(PIECES)),
            sems(len(PIECES) * NY),
            pltpu.SemaphoreType.DMA((9,)),
        ],
        compiler_params=pltpu.CompilerParams(
            collective_id=0, has_side_effects=True, vmem_limit_bytes=56 * 1024 * 1024
        ),
        name="attend",
    )(patches, patch_weight, query_proj, key_proj, value_proj, qkv_weight.transpose(1, 0, 2))
    return (feature_grad, latent_grad)


def solution(mesh):
    split = Mesh(mesh.devices.reshape(SIZES), AXES)
    ty, tx = ("zl", "core"), ("y", "x", "zh")
    placed = (
        P(None, ty, tx, None),
        P(None, ty, tx, None),
        P(),
        P(),
        P(),
        P(None, ty),
        P(tx, ty),
        P(tx, ty),
        P(tx, ty),
        P(tx, None, ty),
    )
    return jax.shard_map(
        body,
        mesh=split,
        in_specs=placed,
        out_specs=(P(None, ty, tx, None), P(tx, ty)),
        check_vma=False,
    )
```

```python
import jax
import jax.numpy as jnp
from jax import lax
from jax.experimental import pallas as pl
from jax.experimental.pallas import tpu as pltpu
from jax.sharding import Mesh
from jax.sharding import PartitionSpec as P

HEAD_DIM = 128

BF = jnp.bfloat16
F32 = jnp.float32
MESH = pl.DeviceIdType.MESH
NN = (((1,), (0,)), ((), ()))
NT = (((1,), (1,)), ((), ()))
TN = (((0,), (0,)), ((), ()))
AXES = ("zl", "core", "y", "x", "zh")
SIZES = (2, 2, 4, 4, 2)
NX, NY, NZ, TY = 4, 4, 2, 4
NK = NX * NZ
HEADS, TOK, COLS = 5, 128, 640
FULL = NX * NY * TOK
LAST = NY * TOK
QUERIES = FULL + LAST
KEYS = NK * TOK
CHUNK = 256
FULL_CHUNKS = FULL // CHUNK
CHUNKS = QUERIES // CHUNK
ROWS_W = 160
CUT_W = 64
OUT = NK * ROWS_W
HALF = OUT // 2
PIECES = ((0, 256), (256, 256), (512, 128))
PATCH = 3072
FACTOR = HEAD_DIM ** (-0.5)
LOG2E = 1.4426950408889634


CH, FINE = 384, 192
AROUND = ((-1, 0), (1, 0), (0, -1), (0, 1), (-1, -1), (-1, 1), (1, -1), (1, 1))
ACROSS = (1, 0, 3, 2, 7, 6, 5, 4)
COLUMNS = NY * NX * NZ


def mm(one, two, dims=NN):
    return lax.dot_general(one, two, dims, preferred_element_type=F32)


def wide(tile):
    return tile.astype(F32)


def whole_kernel(
    fine, preact, gain, up_w, mid_w, patch_w, query, key, value, weight, feature, out,
    g_in, gf, vf, uw, mw, mf, ff, ps, fs_row, fs_col, fs_cor, fr_row, fr_col, fr_cor,
    ms_row, ms_col, ms_cor, mr_row, mr_col, mr_cor, sem_hf, sem_hm,
    p_all, pw, q_all, k_all, v_all, g_own, g_all, w_all, probs, gp, stat_s, stat_r, dot_s, dot_r,
    dq_s, dq_r, dl_r, dk_s, dk_r, dv_s, dv_r, a_all, part, pair, red,
    sem_p, sem_q, sem_k, sem_v, sem_w, sem_g, sem_st, sem_rd, sem_dq, sem_dk, sem_dv, sem_a, sem_c, sem_o, sem_l,
):
    zl, core, y, x, zh = [lax.axis_index(name) for name in AXES]
    c = zl * 2 + core

    def at(dty=0, dy=0, dx=0, dz=0):
        ty = lax.rem(c + dty, TY)
        return (ty // 2, lax.rem(ty, 2), lax.rem(y + dy, NY), lax.rem(x + dx, NX), lax.rem(zh + dz, NZ))

    partner = (zl, 1 - core, y, x, zh)

    def rows(index, size=TOK, base=0):
        return pl.ds(pl.multiple_of(index * size + base, 32), size)

    def cols(h):
        return pl.ds(pl.multiple_of(h * HEAD_DIM, HEAD_DIM), HEAD_DIM)

    def push(src, dst, sems, index, target, arrives=None):
        return pltpu.make_async_remote_copy(
            src_ref=src, dst_ref=dst, send_sem=sems.at[0, index],
            recv_sem=sems.at[1, index if arrives is None else arrives],
            device_id=target, device_id_type=MESH,
        )

    def start(copies):
        for copy in copies:
            copy.start()

    def arrived(copies):
        for copy in copies:
            copy.wait_recv()

    greet = [at(dty=a, dy=b) for a in range(TY) for b in range(NY) if a or b]
    greet += [at(dy=a, dx=b) for a in range(NY) for b in range(1, NX)]
    greet += [at(dx=a, dz=1) for a in range(NX)]
    place = (y * NX + x) * NZ + zh

    def neighbour(i):
        ty = lax.rem(c + AROUND[i][0] + TY, TY)
        t = lax.rem(place + AROUND[i][1] + COLUMNS, COLUMNS)
        return (ty // 2, lax.rem(ty, 2), t // NK, lax.rem(t // NZ, NX), lax.rem(t, NZ))

    def exists(i):
        ty, t = c + AROUND[i][0], place + AROUND[i][1]
        return (ty >= 0) & (ty < TY) & (t >= 0) & (t < COLUMNS)

    def halo_start(made, got, sems):
        for i in range(8):
            @pl.when(exists(i))
            def _():
                push(made[i], got[ACROSS[i]], sems, i, neighbour(i), ACROSS[i]).start()

            @pl.when(jnp.logical_not(exists(i)))
            def _():
                got[i][...] = jnp.zeros(got[i].shape, F32)

    def halo_wait(made, got, sems, sent=False):
        for i in range(8):
            @pl.when(exists(i))
            def _():
                copy = push(made[i], got[i], sems, i, neighbour(i), i)
                if sent:
                    copy.wait_send()
                else:
                    copy.wait_recv()

    greet += [neighbour(i) for i in range(2, 8)]
    barrier = pltpu.get_barrier_semaphore()
    for other in greet:
        pl.semaphore_signal(barrier, inc=1, device_id=other, device_id_type=MESH)

    plane = y * NX + x
    line = x * NZ + zh
    local = [
        pltpu.make_async_copy(patch_w, pw, sem_l.at[1]),
        pltpu.make_async_copy(query.at[:, cols(x)], q_all.at[rows(plane)], sem_l.at[2]),
        pltpu.make_async_copy(query.at[:, cols(NX)], q_all.at[rows(y, base=FULL)], sem_l.at[3]),
        pltpu.make_async_copy(key.at[:, cols(x)], k_all.at[rows(line)], sem_l.at[4]),
        pltpu.make_async_copy(key.at[:, cols(NX)], k_all.at[rows(line, base=KEYS)], sem_l.at[5]),
        pltpu.make_async_copy(value.at[:, cols(x)], v_all.at[rows(line)], sem_l.at[6]),
        pltpu.make_async_copy(value.at[:, cols(NX)], v_all.at[rows(line, base=KEYS)], sem_l.at[7]),
        pltpu.make_async_copy(weight, w_all.at[:, rows(line, ROWS_W)], sem_l.at[8]),
    ]
    of_conv = [
        pltpu.make_async_copy(fine, g_in, sem_l.at[0]),
        pltpu.make_async_copy(up_w.at[pl.ds(1, 2)], uw, sem_l.at[9]),
        pltpu.make_async_copy(mid_w.at[pl.ds(1, 2)], mw, sem_l.at[10]),
    ]
    start(of_conv)
    start(local)

    of_conv[0].wait()
    lanes = ((0, 0, HEAD_DIM), (1, HEAD_DIM, FINE - HEAD_DIM))
    for k, first, size in lanes:
        span = slice(first, first + size)
        gf[k, :, 0:16, 1, 8:24, :size] = wide(g_in[:, :, 0, :, span])
        gf[k, :, 1:17, 0, 8:24, :size] = wide(g_in[:, :, 1, :, span])
        for side, col in ((0, 8), (1, 23)):
            fs_col[side, :, :, 0, :, span] = gf[k, :, 0:16, 1, col : col + 1, :size]
            fs_col[side, :, :, 1, :, span] = gf[k, :, 1:17, 0, col : col + 1, :size]
            fs_cor[side, :, :, span] = gf[k, :, 0, 1, col : col + 1, :size]
            fs_cor[2 + side, :, :, span] = gf[k, :, 16, 0, col : col + 1, :size]
    fs_row[0] = wide(g_in[:, 0, 0])
    fs_row[1] = wide(g_in[:, 15, 1])
    pl.semaphore_wait(barrier, len(greet))
    f_made = [fs_row.at[0], fs_row.at[1], fs_col.at[0], fs_col.at[1]] + [fs_cor.at[i] for i in range(4)]
    f_got = [fr_row.at[0], fr_row.at[1], fr_col.at[0], fr_col.at[1]] + [fr_cor.at[i] for i in range(4)]
    halo_start(f_made, f_got, sem_hf)

    def to_queries(src, dst, sems):
        copies = []
        for dy in range(NY):
            for dx in range(NX):
                if dy or dx:
                    head = cols(lax.rem(x + dx, NX))
                    copies.append(push(src.at[:, head], dst.at[rows(plane)], sems, dy * NX + dx, at(dy=dy, dx=dx)))
            if dy:
                copies.append(push(src.at[:, cols(NX)], dst.at[rows(y, base=FULL)], sems, NY * NX + dy, at(dy=dy)))
        return copies

    def to_keys(src, dst, sems):
        copies = []
        for dz in range(NZ):
            for dx in range(NX):
                if dz or dx:
                    head = cols(lax.rem(x + dx, NX))
                    target = at(dx=dx, dz=dz)
                    slot = 2 * (dx * NZ + dz)
                    copies.append(push(src.at[:, head], dst.at[rows(line)], sems, slot, target))
                    copies.append(push(src.at[:, cols(NX)], dst.at[rows(line, base=KEYS)], sems, slot + 1, target))
        return copies

    own_p = p_all.at[rows(c, 32)]
    to_p = [push(own_p, own_p, sem_p, d, at(dty=d)) for d in range(1, TY)]
    to_k = to_keys(key, k_all, sem_k)
    to_q = to_queries(query, q_all, sem_q)
    to_v = to_keys(value, v_all, sem_v)
    mine = w_all.at[:, rows(line, ROWS_W)]
    to_w = [push(weight, mine, sem_w, d, at(dx=d)) for d in range(1, NX)]
    to_w.append(push(weight, mine, sem_w, 0, at(dz=1)))
    start(to_k + to_q + to_v + to_w)
    beside = w_all.at[:, pl.ds(pl.multiple_of((x * NZ + 1 - zh) * ROWS_W, 32), CUT_W)]
    on_x = [push(beside, beside, sem_w, NX + d, at(dx=d)) for d in range(1, NX)]
    on_z = []
    for d in range(1, NX):
        first = lax.rem(x - d + NX, NX) * NZ + zh
        below = w_all.at[:, pl.ds(pl.multiple_of(first * ROWS_W + CUT_W, 32), ROWS_W - CUT_W)]
        on_z.append(push(below, below, sem_w, 2 * NX + d, at(dz=1)))

    halo_wait(f_made, f_got, sem_hf)
    for k, first, size in lanes:
        span = slice(first, first + size)
        gf[k, :, 0, 0, 8:24, :size] = fr_row[0, :, :, span]
        gf[k, :, 16, 1, 8:24, :size] = fr_row[1, :, :, span]
        for side, col in ((0, 7), (1, 24)):
            gf[k, :, 0:16, 1, col : col + 1, :size] = fr_col[side, :, :, 0, :, span]
            gf[k, :, 1:17, 0, col : col + 1, :size] = fr_col[side, :, :, 1, :, span]
            gf[k, :, 0, 0, col : col + 1, :size] = fr_cor[side, :, :, span]
            gf[k, :, 16, 1, col : col + 1, :size] = fr_cor[2 + side, :, :, span]
        for f in range(2):
            four = [gf[k, f, :, :, pl.ds(7 + s, 8, stride=2), :][..., :size] for s in range(4)]
            for tap in range(3):
                vf[tap, f, :, :, :, span] = four[2 - tap] + four[3 - tap]
    of_conv[1].wait()

    def causal(cells, weights, dims):
        own = later = None
        for tap in range(9):
            both = jnp.concatenate([cells(0, tap), cells(1, tap)], axis=0)
            one = mm(both, weights[1, tap], dims)
            two = mm(both[TOK:], weights[0, tap], dims)
            own = one if own is None else own + one
            later = two if later is None else later + two
        return own[:TOK] + later, own[TOK:]

    def fine_cells(f, tap):
        b, col = tap // 3, tap % 3
        one = vf[col, f, 0:16, 1] if b else vf[col, f, 1:17, 0]
        two = (vf[col, f, 1:17, 1], vf[col, f, 1:17, 0], vf[col, f, 0:16, 0])[b]
        return (one + two).reshape(TOK, FINE).astype(BF)

    for f, pooled in enumerate(causal(fine_cells, uw, NN)):
        z = gain[...] * wide(preact[f].reshape(TOK, CH))
        s = 1.0 / (1.0 + jnp.exp(-z))
        mid = (pooled * gain[...] * s * (1.0 + z * (1.0 - s))).astype(BF)
        mf[f, 1:17, 8:16, :] = wide(mid).reshape(16, 8, CH)
    ms_row[0] = mf[:, 1, 8:16, :]
    ms_row[1] = mf[:, 16, 8:16, :]
    for side, col in ((0, 8), (1, 15)):
        ms_col[side] = mf[:, 1:17, col : col + 1, :]
        ms_cor[side] = mf[:, 1, col : col + 1, :]
        ms_cor[2 + side] = mf[:, 16, col : col + 1, :]
    m_made = [ms_row.at[0], ms_row.at[1], ms_col.at[0], ms_col.at[1]] + [ms_cor.at[i] for i in range(4)]
    m_got = [mr_row.at[0], mr_row.at[1], mr_col.at[0], mr_col.at[1]] + [mr_cor.at[i] for i in range(4)]
    halo_start(m_made, m_got, sem_hm)
    for copy in local + of_conv[2:]:
        copy.wait()
    halo_wait(m_made, m_got, sem_hm)
    mf[:, 0, 8:16, :] = mr_row[0]
    mf[:, 17, 8:16, :] = mr_row[1]
    for side, col in ((0, 7), (1, 16)):
        mf[:, 1:17, col : col + 1, :] = mr_col[side]
        mf[:, 0, col : col + 1, :] = mr_cor[side]
        mf[:, 17, col : col + 1, :] = mr_cor[2 + side]

    def mid_cells(f, tap):
        b, col = tap // 3, tap % 3
        return mf[f, 2 - b : 18 - b, 9 - col : 17 - col, :].reshape(TOK, CH).astype(BF)

    for f, total in enumerate(causal(mid_cells, mw, NT)):
        low = total.astype(BF)
        feature[f] = low.reshape(16, 8, CH)
        for k in range(3):
            ff[k, f] = wide(low[:, k * HEAD_DIM : (k + 1) * HEAD_DIM]).reshape(16, 8, HEAD_DIM)
    for t in range(2):
        for u in range(2):
            for w in range(2):
                first = ((t * 2 + u) * 2 + w) * CH
                for k in range(3):
                    span = slice(first + k * HEAD_DIM, first + (k + 1) * HEAD_DIM)
                    for p in range(8):
                        ps[p * 4 : p * 4 + 4, span] = ff[k, t, 2 * p + u, pl.ds(w, 4, stride=2), :]
    p_all[rows(c, 32), :] = ps[...].astype(BF)
    start(to_p)

    arrived(to_p)
    g_own[...] = mm(p_all[...], pw[...]).astype(BF)
    to_g = to_queries(g_own, g_all, sem_g)
    start(to_g)
    g_all[rows(plane), :] = g_own[:, cols(x)]
    g_all[rows(y, base=FULL), :] = g_own[:, cols(NX)]

    arrived(to_k + to_q)

    def spans(i):
        return rows(i, CHUNK), rows(i // FULL_CHUNKS, KEYS)

    def score_step(i, _):
        span, keys = spans(i)
        s = mm(k_all[keys, :], q_all[span, :], NT) * (FACTOR * LOG2E)
        peak = jnp.max(s, axis=0, keepdims=True)
        e = jnp.exp2(s - peak)
        stat_s[0, :, span] = peak
        stat_s[1, :, span] = jnp.sum(e, axis=0, keepdims=True)
        probs[:, span] = e.astype(BF)
        return 0

    lax.fori_loop(0, CHUNKS, score_step, 0)
    to_st = [push(stat_s, stat_r.at[y], sem_st, d, at(dy=d)) for d in range(1, NY)]
    start(to_st)
    stat_r[y] = stat_s[...]
    arrived(to_st)

    def share_step(i, _):
        span, _ = spans(i)
        top = stat_r[0, 0, :, span]
        for j in range(1, NY):
            top = jnp.maximum(top, stat_r[j, 0, :, span])
        total = jnp.zeros_like(top)
        for j in range(NY):
            total = total + stat_r[j, 1, :, span] * jnp.exp2(stat_r[j, 0, :, span] - top)
        share = jnp.exp2(stat_s[0, :, span] - top) / total
        probs[:, span] = (wide(probs[:, span]) * share).astype(BF)
        return 0

    lax.fori_loop(0, CHUNKS, share_step, 0)
    arrived(to_v + to_g)

    def grad_step(i, _):
        span, keys = spans(i)
        g = mm(v_all[keys, :], g_all[span, :], NT)
        dot_s[:, span] = jnp.sum(wide(probs[:, span]) * g, axis=0, keepdims=True)
        gp[:, span] = g.astype(BF)
        return 0

    lax.fori_loop(0, CHUNKS, grad_step, 0)
    to_rd = [push(dot_s, dot_r.at[y], sem_rd, d, at(dy=d)) for d in range(1, NY)]
    start(to_rd)
    dot_r[y] = dot_s[...]

    def key_copies(d, made, got, sems):
        copies = []
        block = lax.rem(x + d, NX) * NZ
        for dz in range(NZ):
            if d or dz:
                there = block + lax.rem(zh + dz, NZ)
                for k in range(2):
                    copies.append(
                        push(made.at[k, rows(there)], got.at[line, k], sems, 2 * (d * NZ + dz) + k, at(dx=d, dz=dz))
                    )
        return copies

    def key_sums(left, right, made, got, sems, scale):
        for d in (2, 1, 3, 0):
            block = rows(lax.rem(x + d, NX), NZ * TOK)
            made[0, block, :] = (scale * mm(left[block, :FULL], right[:FULL, :])).astype(BF)
            made[1, block, :] = (scale * mm(left[block, FULL:], right[FULL:, :])).astype(BF)
            start(key_copies(d, made, got, sems))
        got[line] = made[:, rows(line), :]

    def all_key_copies(made, got, sems):
        return [copy for d in range(NX) for copy in key_copies(d, made, got, sems)]

    key_sums(probs, g_all, dv_s, dv_r, sem_dv, 1.0)
    to_dv = all_key_copies(dv_s, dv_r, sem_dv)
    arrived(to_rd)
    arrived(to_w)
    start(on_x + on_z)

    def query_copies(d):
        copies = []
        there = lax.rem(y + d, NY)
        for dx in range(NX):
            if d or dx:
                block = rows(there * NX + lax.rem(x + dx, NX))
                copies.append(push(dq_s.at[block], dq_r.at[plane], sem_dq, d * NX + dx, at(dy=d, dx=dx)))
        return copies

    def last_copy(d):
        block = rows(lax.rem(y + d, NY), base=FULL)
        return push(dq_s.at[block], dl_r.at[y], sem_dq, NY * NX + d, at(dy=d))

    def query_step(i, _):
        span, keys = spans(i)
        dot = dot_r[0, :, span]
        for j in range(1, NY):
            dot = dot + dot_r[j, :, span]
        ds = (wide(probs[:, span]) * (wide(gp[:, span]) - dot)).astype(BF)
        gp[:, span] = ds
        dq_s[span, :] = (FACTOR * mm(ds, k_all[keys, :], TN)).astype(BF)
        return 0

    for d in (2, 1, 3, 0):
        first = lax.rem(y + d, NY) * 2
        lax.fori_loop(first, first + 2, query_step, 0)
        start(query_copies(d))
    lax.fori_loop(FULL_CHUNKS, CHUNKS, query_step, 0)
    to_dl = [last_copy(d) for d in range(1, NY)]
    start(to_dl)
    dq_r[plane] = dq_s[rows(plane), :]
    dl_r[y] = dq_s[rows(y, base=FULL), :]
    key_sums(gp, q_all, dk_s, dk_r, sem_dk, FACTOR)
    to_dk = all_key_copies(dk_s, dk_r, sem_dk)
    to_dq = [copy for d in range(NY) for copy in query_copies(d)]

    def key_total(part_index, got):
        for h in range(NX):
            total = wide(got[h * NZ, 0])
            for j in range(1, NZ):
                total = total + wide(got[h * NZ + j, 0])
            a_all[part_index, rows(y), h * HEAD_DIM : (h + 1) * HEAD_DIM] = total.astype(BF)
        total = wide(got[0, 1])
        for j in range(1, NK):
            total = total + wide(got[j, 1])
        a_all[part_index, rows(y), NX * HEAD_DIM :] = total.astype(BF)

    def a_copies(k):
        mine = a_all.at[k, rows(y)]
        return [push(mine, mine, sem_a, k * NY + d, at(dy=d)) for d in range(1, NY)]

    to_a = [a_copies(k) for k in range(3)]
    arrived(to_dv)
    key_total(2, dv_r)
    start(to_a[2])
    arrived(to_dq + to_dl)
    for h in range(NX):
        total = wide(dq_r[h])
        for j in range(1, NY):
            total = total + wide(dq_r[j * NX + h])
        a_all[0, rows(y), h * HEAD_DIM : (h + 1) * HEAD_DIM] = total.astype(BF)
    total = wide(dl_r[0])
    for j in range(1, NY):
        total = total + wide(dl_r[j])
    a_all[0, rows(y), NX * HEAD_DIM :] = total.astype(BF)
    start(to_a[0])
    arrived(to_dk)
    key_total(1, dk_r)
    start(to_a[1])
    arrived(on_x + on_z)
    for k in (2, 0, 1):
        arrived(to_a[k])

    def project(first, size):
        span = pl.ds(pl.multiple_of(first, HEAD_DIM), size)
        total = mm(a_all[0], w_all[0, span, :], NT)
        total = total + mm(a_all[1], w_all[1, span, :], NT)
        return total + mm(a_all[2], w_all[2, span, :], NT)

    to_c = []
    for n, (first, size) in enumerate(PIECES):
        part[:, first : first + size] = project((1 - core) * HALF + first, size).astype(BF)
        span = pl.ds(first, size)
        copy = push(part.at[:, span], pair.at[:, span], sem_c, n, partner)
        copy.start()
        to_c.append(copy)

    def out_copy(n, d):
        first, size = PIECES[n]
        to = lax.rem(y + d, NY)
        span = pl.ds(pl.multiple_of(core * HALF + first, HEAD_DIM), size)
        return push(
            pair.at[rows(to), pl.ds(first, size)], red.at[zl, :, span], sem_o, n * NY + d,
            (y // 2, lax.rem(y, 2), to, x, zh), n * NY + c,
        )

    for n, (first, size) in enumerate(PIECES):
        total = project(core * HALF + first, size)
        to_c[n].wait_recv()
        span = pl.ds(first, size)
        pair[:, span] = (total + wide(pair[:, span])).astype(BF)
        for d in (2, 1, 3):
            out_copy(n, d).start()

        @pl.when(c == y)
        def _():
            red[zl, :, pl.ds(pl.multiple_of(core * HALF + first, HEAD_DIM), size)] = pair[rows(y), span]

        @pl.when(c != y)
        def _():
            out_copy(n, 0).start()

    for n, (first, size) in enumerate(PIECES):
        for other in range(TY):
            @pl.when((c != y) | (c != other))
            def _():
                push(
                    pair.at[rows(0), pl.ds(first, size)], red.at[other // 2, :, pl.ds((other % 2) * HALF + first, size)],
                    sem_o, n * NY, at(dy=1), n * NY + other,
                ).wait_recv()
        for half in range(2):
            span = pl.ds(half * HALF + first, size)
            out[:, span] = (wide(red[0, :, span]) + wide(red[1, :, span])).astype(BF)

    done = to_p + to_k + to_q + to_v + to_w + on_x + on_z + to_g + to_st + to_rd + to_dv + to_dq + to_dl + to_dk
    for copy in done + to_a[0] + to_a[1] + to_a[2] + to_c:
        copy.wait_send()
    halo_wait(f_made, f_got, sem_hf, sent=True)
    halo_wait(m_made, m_got, sem_hm, sent=True)
    for n in range(len(PIECES)):
        for d in range(1, NY):
            out_copy(n, d).wait_send()

        @pl.when(c != y)
        def _():
            out_copy(n, 0).wait_send()


def body(
    out_grad,
    preact,
    norm_gain,
    mid_weight,
    up_weight,
    patch_weight,
    query_proj,
    key_proj,
    value_proj,
    qkv_weight,
):
    any_space = pl.BlockSpec(memory_space=pl.ANY)

    def sems(count):
        return pltpu.SemaphoreType.DMA((2, count))

    in_vmem = pl.BlockSpec(memory_space=pltpu.VMEM)

    def strips(count, *shape):
        return pltpu.VMEM((count, 2) + shape, F32)

    return pl.pallas_call(
        whole_kernel,
        out_shape=(
            jax.ShapeDtypeStruct((2, 16, 8, CH), BF),
            jax.ShapeDtypeStruct((TOK, OUT), BF),
        ),
        in_specs=[any_space] + [in_vmem] * 2 + [any_space] * 7,
        out_specs=(in_vmem, in_vmem),
        scratch_shapes=[
            pltpu.VMEM((2, 16, 2, 16, FINE), BF),
            pltpu.VMEM((2, 2, 17, 2, 32, HEAD_DIM), F32),
            pltpu.VMEM((3, 2, 17, 2, 8, FINE), F32),
            pltpu.VMEM((2, 9, FINE, CH), BF),
            pltpu.VMEM((2, 9, CH, CH), BF),
            pltpu.VMEM((2, 18, 24, CH), F32),
            pltpu.VMEM((3, 2, 16, 8, HEAD_DIM), F32),
            pltpu.VMEM((32, PATCH), F32),
            strips(2, 16, FINE),
            strips(2, 16, 2, 1, FINE),
            strips(4, 1, FINE),
            strips(2, 16, FINE),
            strips(2, 16, 2, 1, FINE),
            strips(4, 1, FINE),
            strips(2, 8, CH),
            strips(2, 16, 1, CH),
            strips(4, 1, CH),
            strips(2, 8, CH),
            strips(2, 16, 1, CH),
            strips(4, 1, CH),
            sems(8),
            sems(8),
            pltpu.VMEM((TOK, PATCH), BF),
            pltpu.VMEM((PATCH, COLS), BF),
            pltpu.VMEM((QUERIES, HEAD_DIM), BF),
            pltpu.VMEM((2 * KEYS, HEAD_DIM), BF),
            pltpu.VMEM((2 * KEYS, HEAD_DIM), BF),
            pltpu.VMEM((TOK, COLS), BF),
            pltpu.VMEM((QUERIES, HEAD_DIM), BF),
            pltpu.VMEM((3, OUT, COLS), BF),
            pltpu.VMEM((KEYS, QUERIES), BF),
            pltpu.VMEM((KEYS, QUERIES), BF),
            pltpu.VMEM((2, 1, QUERIES), F32),
            pltpu.VMEM((NY, 2, 1, QUERIES), F32),
            pltpu.VMEM((1, QUERIES), F32),
            pltpu.VMEM((NY, 1, QUERIES), F32),
            pltpu.VMEM((QUERIES, HEAD_DIM), BF),
            pltpu.VMEM((NY * NX, TOK, HEAD_DIM), BF),
            pltpu.VMEM((NY, TOK, HEAD_DIM), BF),
            pltpu.VMEM((2, KEYS, HEAD_DIM), BF),
            pltpu.VMEM((NK, 2, TOK, HEAD_DIM), BF),
            pltpu.VMEM((2, KEYS, HEAD_DIM), BF),
            pltpu.VMEM((NK, 2, TOK, HEAD_DIM), BF),
            pltpu.VMEM((3, LAST, COLS), BF),
            pltpu.VMEM((LAST, HALF), BF),
            pltpu.VMEM((LAST, HALF), BF),
            pltpu.VMEM((2, TOK, OUT), BF),
            sems(TY),
            sems(NY * NX + NY),
            sems(2 * NK),
            sems(2 * NK),
            sems(3 * NX),
            sems(NY * NX + NY),
            sems(NY),
            sems(NY),
            sems(NY * NX + NY),
            sems(2 * NK),
            sems(2 * NK),
            sems(3 * NY),
            sems(len(PIECES)),
            sems(len(PIECES) * NY),
            pltpu.SemaphoreType.DMA((11,)),
        ],
        compiler_params=pltpu.CompilerParams(
            collective_id=0, has_side_effects=True, vmem_limit_bytes=56 * 1024 * 1024
        ),
        name="whole",
    )(
        out_grad.reshape(2, 16, 2, 16, FINE),
        preact,
        norm_gain.reshape(1, CH),
        up_weight.transpose(0, 1, 2, 4, 3).reshape(3, 9, FINE, CH),
        mid_weight.reshape(3, 9, CH, CH),
        patch_weight,
        query_proj,
        key_proj,
        value_proj,
        qkv_weight.transpose(1, 0, 2),
    )


def solution(mesh):
    split = Mesh(mesh.devices.reshape(SIZES), AXES)
    ty, tx = ("zl", "core"), ("y", "x", "zh")
    placed = (
        P(None, ty, tx, None),
        P(None, ty, tx, None),
        P(),
        P(),
        P(),
        P(None, ty),
        P(tx, ty),
        P(tx, ty),
        P(tx, ty),
        P(tx, None, ty),
    )
    return jax.shard_map(
        body,
        mesh=split,
        in_specs=placed,
        out_specs=(P(None, ty, tx, None), P(tx, ty)),
        check_vma=False,
    )
```

```python
import jax
import jax.numpy as jnp
from jax import lax
from jax.experimental import pallas as pl
from jax.experimental.pallas import tpu as pltpu
from jax.sharding import Mesh
from jax.sharding import PartitionSpec as P

HEAD_DIM = 128

BF = jnp.bfloat16
F32 = jnp.float32
MESH = pl.DeviceIdType.MESH
NN = (((1,), (0,)), ((), ()))
NT = (((1,), (1,)), ((), ()))
TN = (((0,), (0,)), ((), ()))
AXES = ("zl", "core", "y", "x", "zh")
SIZES = (2, 2, 4, 4, 2)
NX, NY, NZ, TY = 4, 4, 2, 4
NK = NX * NZ
HEADS, TOK, COLS = 5, 128, 640
FULL = NX * NY * TOK
LAST = NY * TOK
QUERIES = FULL + LAST
KEYS = NK * TOK
CHUNK = 256
FULL_CHUNKS = FULL // CHUNK
CHUNKS = QUERIES // CHUNK
ROWS_W = 160
CUT_W = 48
OUT = NK * ROWS_W
HALF = OUT // 2
PIECES = ((0, 256), (256, 256), (512, 128))
PATCH = 3072
FACTOR = HEAD_DIM ** (-0.5)
LOG2E = 1.4426950408889634


CH, FINE = 384, 192
AROUND = ((-1, 0), (1, 0), (0, -1), (0, 1), (-1, -1), (-1, 1), (1, -1), (1, 1))
ACROSS = (1, 0, 3, 2, 7, 6, 5, 4)
COLUMNS = NY * NX * NZ


def mm(one, two, dims=NN):
    return lax.dot_general(one, two, dims, preferred_element_type=F32)


def wide(tile):
    return tile.astype(F32)


def whole_kernel(
    fine, preact, gain, up_w, mid_w, patch_w, query, key, value, weight, feature, out,
    g_in, gf, vf, uw, mw, mf, ff, ps, fs_row, fs_col, fs_cor, fr_row, fr_col, fr_cor,
    ms_row, ms_col, ms_cor, mr_row, mr_col, mr_cor, sem_hf, sem_hm,
    p_all, pw, q_all, k_all, v_all, g_own, g_all, w_all, probs, gp, stat_s, stat_r, dot_s, dot_r,
    dq_s, dq_r, dl_r, dk_s, dk_r, dv_s, dv_r, a_all, part, pair, red,
    sem_p, sem_q, sem_k, sem_v, sem_w, sem_g, sem_st, sem_rd, sem_dq, sem_dk, sem_dv, sem_a, sem_c, sem_o, sem_l,
):
    zl, core, y, x, zh = [lax.axis_index(name) for name in AXES]
    c = zl * 2 + core

    def at(dty=0, dy=0, dx=0, dz=0):
        ty = lax.rem(c + dty, TY)
        return (ty // 2, lax.rem(ty, 2), lax.rem(y + dy, NY), lax.rem(x + dx, NX), lax.rem(zh + dz, NZ))

    partner = (zl, 1 - core, y, x, zh)

    def rows(index, size=TOK, base=0):
        return pl.ds(pl.multiple_of(index * size + base, 32), size)

    def cols(h):
        return pl.ds(pl.multiple_of(h * HEAD_DIM, HEAD_DIM), HEAD_DIM)

    def push(src, dst, sems, index, target, arrives=None):
        return pltpu.make_async_remote_copy(
            src_ref=src, dst_ref=dst, send_sem=sems.at[0, index],
            recv_sem=sems.at[1, index if arrives is None else arrives],
            device_id=target, device_id_type=MESH,
        )

    def start(copies):
        for copy in copies:
            copy.start()

    def arrived(copies):
        for copy in copies:
            copy.wait_recv()

    greet = [at(dty=a, dy=b) for a in range(TY) for b in range(NY) if a or b]
    greet += [at(dy=a, dx=b) for a in range(NY) for b in range(1, NX)]
    greet += [at(dx=a, dz=1) for a in range(NX)]
    place = (y * NX + x) * NZ + zh

    def neighbour(i):
        ty = lax.rem(c + AROUND[i][0] + TY, TY)
        t = lax.rem(place + AROUND[i][1] + COLUMNS, COLUMNS)
        return (ty // 2, lax.rem(ty, 2), t // NK, lax.rem(t // NZ, NX), lax.rem(t, NZ))

    def exists(i):
        ty, t = c + AROUND[i][0], place + AROUND[i][1]
        return (ty >= 0) & (ty < TY) & (t >= 0) & (t < COLUMNS)

    def halo_start(made, got, sems):
        for i in range(8):
            @pl.when(exists(i))
            def _():
                push(made[i], got[ACROSS[i]], sems, i, neighbour(i), ACROSS[i]).start()

            @pl.when(jnp.logical_not(exists(i)))
            def _():
                got[i][...] = jnp.zeros(got[i].shape, F32)

    def halo_wait(made, got, sems, sent=False):
        for i in range(8):
            @pl.when(exists(i))
            def _():
                copy = push(made[i], got[i], sems, i, neighbour(i), i)
                if sent:
                    copy.wait_send()
                else:
                    copy.wait_recv()

    greet += [neighbour(i) for i in range(2, 8)]
    barrier = pltpu.get_barrier_semaphore()
    for other in greet:
        pl.semaphore_signal(barrier, inc=1, device_id=other, device_id_type=MESH)

    plane = y * NX + x
    line = x * NZ + zh
    local = [
        pltpu.make_async_copy(patch_w, pw, sem_l.at[1]),
        pltpu.make_async_copy(query.at[:, cols(x)], q_all.at[rows(plane)], sem_l.at[2]),
        pltpu.make_async_copy(query.at[:, cols(NX)], q_all.at[rows(y, base=FULL)], sem_l.at[3]),
        pltpu.make_async_copy(key.at[:, cols(x)], k_all.at[rows(line)], sem_l.at[4]),
        pltpu.make_async_copy(key.at[:, cols(NX)], k_all.at[rows(line, base=KEYS)], sem_l.at[5]),
        pltpu.make_async_copy(value.at[:, cols(x)], v_all.at[rows(line)], sem_l.at[6]),
        pltpu.make_async_copy(value.at[:, cols(NX)], v_all.at[rows(line, base=KEYS)], sem_l.at[7]),
        pltpu.make_async_copy(weight, w_all.at[:, rows(line, ROWS_W)], sem_l.at[8]),
    ]
    of_conv = [
        pltpu.make_async_copy(fine, g_in, sem_l.at[0]),
        pltpu.make_async_copy(up_w.at[pl.ds(1, 2)], uw, sem_l.at[9]),
        pltpu.make_async_copy(mid_w.at[pl.ds(1, 2)], mw, sem_l.at[10]),
    ]
    start(of_conv)
    start(local)

    of_conv[0].wait()
    lanes = ((0, 0, HEAD_DIM), (1, HEAD_DIM, FINE - HEAD_DIM))
    for k, first, size in lanes:
        span = slice(first, first + size)
        gf[k, :, 0:16, 1, 8:24, :size] = wide(g_in[:, :, 0, :, span])
        gf[k, :, 1:17, 0, 8:24, :size] = wide(g_in[:, :, 1, :, span])
        for side, col in ((0, 8), (1, 23)):
            fs_col[side, :, :, 0, :, span] = gf[k, :, 0:16, 1, col : col + 1, :size]
            fs_col[side, :, :, 1, :, span] = gf[k, :, 1:17, 0, col : col + 1, :size]
            fs_cor[side, :, :, span] = gf[k, :, 0, 1, col : col + 1, :size]
            fs_cor[2 + side, :, :, span] = gf[k, :, 16, 0, col : col + 1, :size]
    fs_row[0] = wide(g_in[:, 0, 0])
    fs_row[1] = wide(g_in[:, 15, 1])
    pl.semaphore_wait(barrier, len(greet))
    f_made = [fs_row.at[0], fs_row.at[1], fs_col.at[0], fs_col.at[1]] + [fs_cor.at[i] for i in range(4)]
    f_got = [fr_row.at[0], fr_row.at[1], fr_col.at[0], fr_col.at[1]] + [fr_cor.at[i] for i in range(4)]
    halo_start(f_made, f_got, sem_hf)

    def to_queries(src, dst, sems):
        copies = []
        for dy in range(NY):
            for dx in range(NX):
                if dy or dx:
                    head = cols(lax.rem(x + dx, NX))
                    copies.append(push(src.at[:, head], dst.at[rows(plane)], sems, dy * NX + dx, at(dy=dy, dx=dx)))
            if dy:
                copies.append(push(src.at[:, cols(NX)], dst.at[rows(y, base=FULL)], sems, NY * NX + dy, at(dy=dy)))
        return copies

    def keys_over_x(src, dst, sems):
        copies = []
        for d in range(1, NX):
            head = cols(lax.rem(x + d, NX))
            copies.append(push(src.at[:, head], dst.at[rows(line)], sems, 2 * d, at(dx=d)))
            copies.append(push(src.at[:, cols(NX)], dst.at[rows(line, base=KEYS)], sems, 2 * d + 1, at(dx=d)))
        return copies

    def keys_over_z(dst, sems, steps):
        copies = []
        for d in steps:
            block = lax.rem(x - d + NX, NX) * NZ + zh
            for k in range(2):
                there = dst.at[rows(block, base=k * KEYS)]
                copies.append(push(there, there, sems, 2 * NX + 2 * d + k, at(dz=1)))
        return copies

    own_p = p_all.at[rows(c, 32)]
    over_z = lax.rem(c + 2, TY)
    far_p = p_all.at[rows(over_z, 32)]
    to_p = [push(own_p, own_p, sem_p, 0, at(dty=2)), push(own_p, own_p, sem_p, 1, partner)]
    on_p = [push(far_p, far_p, sem_p, 2, partner)]
    kx, vx = keys_over_x(key, k_all, sem_k), keys_over_x(value, v_all, sem_v)
    kz, vz = keys_over_z(k_all, sem_k, (1, 2, 3)), keys_over_z(v_all, sem_v, (1, 2, 3))
    own_kz, own_vz = keys_over_z(k_all, sem_k, (0,)), keys_over_z(v_all, sem_v, (0,))
    to_k, to_v = kx + kz + own_kz, vx + vz + own_vz
    to_q = to_queries(query, q_all, sem_q)
    mine = w_all.at[:, rows(line, ROWS_W)]
    to_w = [push(weight, mine, sem_w, d, at(dx=d)) for d in range(1, NX)]
    to_wz = push(weight, mine, sem_w, 0, at(dz=1))
    for copy in local:
        copy.wait()
    start(kx + own_kz)
    beside = w_all.at[:, pl.ds(pl.multiple_of((x * NZ + 1 - zh) * ROWS_W, 16), CUT_W)]
    on_x = [push(beside, beside, sem_w, NX + d, at(dx=d)) for d in range(1, NX)]
    on_z = []
    for d in range(1, NX):
        first = lax.rem(x - d + NX, NX) * NZ + zh
        below = w_all.at[:, pl.ds(pl.multiple_of(first * ROWS_W + CUT_W, 16), ROWS_W - CUT_W)]
        on_z.append(push(below, below, sem_w, 2 * NX + d, at(dz=1)))

    halo_wait(f_made, f_got, sem_hf)
    for k, first, size in lanes:
        span = slice(first, first + size)
        gf[k, :, 0, 0, 8:24, :size] = fr_row[0, :, :, span]
        gf[k, :, 16, 1, 8:24, :size] = fr_row[1, :, :, span]
        for side, col in ((0, 7), (1, 24)):
            gf[k, :, 0:16, 1, col : col + 1, :size] = fr_col[side, :, :, 0, :, span]
            gf[k, :, 1:17, 0, col : col + 1, :size] = fr_col[side, :, :, 1, :, span]
            gf[k, :, 0, 0, col : col + 1, :size] = fr_cor[side, :, :, span]
            gf[k, :, 16, 1, col : col + 1, :size] = fr_cor[2 + side, :, :, span]
        for f in range(2):
            four = [gf[k, f, :, :, pl.ds(7 + s, 8, stride=2), :][..., :size] for s in range(4)]
            for tap in range(3):
                vf[tap, f, :, :, :, span] = four[2 - tap] + four[3 - tap]
    of_conv[1].wait()

    def causal(cells, weights, dims):
        own = later = None
        for tap in range(9):
            both = jnp.concatenate([cells(0, tap), cells(1, tap)], axis=0)
            one = mm(both, weights[1, tap], dims)
            two = mm(both[TOK:], weights[0, tap], dims)
            own = one if own is None else own + one
            later = two if later is None else later + two
        return own[:TOK] + later, own[TOK:]

    def fine_cells(f, tap):
        b, col = tap // 3, tap % 3
        one = vf[col, f, 0:16, 1] if b else vf[col, f, 1:17, 0]
        two = (vf[col, f, 1:17, 1], vf[col, f, 1:17, 0], vf[col, f, 0:16, 0])[b]
        return (one + two).reshape(TOK, FINE).astype(BF)

    scale = gain[...].reshape(1, CH)
    for f, pooled in enumerate(causal(fine_cells, uw, NN)):
        z = scale * wide(preact[f].reshape(TOK, CH))
        s = 1.0 / (1.0 + jnp.exp(-z))
        mid = (pooled * scale * s * (1.0 + z * (1.0 - s))).astype(BF)
        mf[f, 1:17, 8:16, :] = wide(mid).reshape(16, 8, CH)
    ms_row[0] = mf[:, 1, 8:16, :]
    ms_row[1] = mf[:, 16, 8:16, :]
    for side, col in ((0, 8), (1, 15)):
        ms_col[side] = mf[:, 1:17, col : col + 1, :]
        ms_cor[side] = mf[:, 1, col : col + 1, :]
        ms_cor[2 + side] = mf[:, 16, col : col + 1, :]
    m_made = [ms_row.at[0], ms_row.at[1], ms_col.at[0], ms_col.at[1]] + [ms_cor.at[i] for i in range(4)]
    m_got = [mr_row.at[0], mr_row.at[1], mr_col.at[0], mr_col.at[1]] + [mr_cor.at[i] for i in range(4)]
    halo_start(m_made, m_got, sem_hm)
    arrived(kx)
    start(kz + to_q + vx)
    of_conv[2].wait()
    halo_wait(m_made, m_got, sem_hm)
    mf[:, 0, 8:16, :] = mr_row[0]
    mf[:, 17, 8:16, :] = mr_row[1]
    for side, col in ((0, 7), (1, 16)):
        mf[:, 1:17, col : col + 1, :] = mr_col[side]
        mf[:, 0, col : col + 1, :] = mr_cor[side]
        mf[:, 17, col : col + 1, :] = mr_cor[2 + side]

    def mid_cells(f, tap):
        b, col = tap // 3, tap % 3
        return mf[f, 2 - b : 18 - b, 9 - col : 17 - col, :].reshape(TOK, CH).astype(BF)

    for f, total in enumerate(causal(mid_cells, mw, NT)):
        low = total.astype(BF)
        feature[f] = low.reshape(16, 8, CH)
        for k in range(3):
            ff[k, f] = wide(low[:, k * HEAD_DIM : (k + 1) * HEAD_DIM]).reshape(16, 8, HEAD_DIM)
    for t in range(2):
        for u in range(2):
            for w in range(2):
                first = ((t * 2 + u) * 2 + w) * CH
                for k in range(3):
                    span = slice(first + k * HEAD_DIM, first + (k + 1) * HEAD_DIM)
                    for p in range(8):
                        ps[p * 4 : p * 4 + 4, span] = ff[k, t, 2 * p + u, pl.ds(w, 4, stride=2), :]
    p_all[rows(c, 32), :] = ps[...].astype(BF)
    start(to_p)

    arrived(to_p[:1])
    start(on_p)
    arrived(to_p[1:] + on_p)
    g_own[...] = mm(p_all[...], pw[...]).astype(BF)
    to_g = to_queries(g_own, g_all, sem_g)
    start(to_g)
    arrived(vx)
    start(own_vz + vz + [to_wz, to_w[0], to_w[2]])
    g_all[rows(plane), :] = g_own[:, cols(x)]
    g_all[rows(y, base=FULL), :] = g_own[:, cols(NX)]

    arrived(kz + own_kz + to_q)

    def spans(i):
        return rows(i, CHUNK), rows(i // FULL_CHUNKS, KEYS)

    def score_step(i, _):
        span, keys = spans(i)
        s = mm(k_all[keys, :], q_all[span, :], NT) * (FACTOR * LOG2E)
        peak = jnp.max(s, axis=0, keepdims=True)
        e = jnp.exp2(s - peak)
        stat_s[0, :, span] = peak
        stat_s[1, :, span] = jnp.sum(e, axis=0, keepdims=True)
        probs[:, span] = e.astype(BF)
        return 0

    lax.fori_loop(0, CHUNKS, score_step, 0)
    to_st = [push(stat_s, stat_r.at[y], sem_st, d, at(dy=d)) for d in range(1, NY)]
    start(to_st)
    stat_r[y] = stat_s[...]
    arrived(to_st)

    def share_step(i, _):
        span, _ = spans(i)
        top = stat_r[0, 0, :, span]
        for j in range(1, NY):
            top = jnp.maximum(top, stat_r[j, 0, :, span])
        total = jnp.zeros_like(top)
        for j in range(NY):
            total = total + stat_r[j, 1, :, span] * jnp.exp2(stat_r[j, 0, :, span] - top)
        share = jnp.exp2(stat_s[0, :, span] - top) / total
        probs[:, span] = (wide(probs[:, span]) * share).astype(BF)
        return 0

    lax.fori_loop(0, CHUNKS, share_step, 0)
    arrived(vz + own_vz + to_g)

    def grad_step(i, _):
        span, keys = spans(i)
        g = mm(v_all[keys, :], g_all[span, :], NT)
        dot_s[:, span] = jnp.sum(wide(probs[:, span]) * g, axis=0, keepdims=True)
        gp[:, span] = g.astype(BF)
        return 0

    lax.fori_loop(0, CHUNKS, grad_step, 0)
    to_rd = [push(dot_s, dot_r.at[y], sem_rd, d, at(dy=d)) for d in range(1, NY)]
    start(to_rd)
    dot_r[y] = dot_s[...]

    def key_copies(d, made, got, sems):
        copies = []
        block = lax.rem(x + d, NX) * NZ
        for dz in range(NZ):
            if d or dz:
                there = block + lax.rem(zh + dz, NZ)
                for k in range(2):
                    copies.append(
                        push(made.at[k, rows(there)], got.at[line, k], sems, 2 * (d * NZ + dz) + k, at(dx=d, dz=dz))
                    )
        return copies

    def key_sums(left, right, made, got, sems, scale):
        for d in (2, 1, 3, 0):
            block = rows(lax.rem(x + d, NX), NZ * TOK)
            made[0, block, :] = (scale * mm(left[block, :FULL], right[:FULL, :])).astype(BF)
            made[1, block, :] = (scale * mm(left[block, FULL:], right[FULL:, :])).astype(BF)
            start(key_copies(d, made, got, sems))
        got[line] = made[:, rows(line), :]

    def all_key_copies(made, got, sems):
        return [copy for d in range(NX) for copy in key_copies(d, made, got, sems)]

    key_sums(probs, g_all, dv_s, dv_r, sem_dv, 1.0)
    to_dv = all_key_copies(dv_s, dv_r, sem_dv)
    arrived(to_rd)

    def query_copies(d):
        copies = []
        there = lax.rem(y + d, NY)
        for dx in range(NX):
            if d or dx:
                block = rows(there * NX + lax.rem(x + dx, NX))
                copies.append(push(dq_s.at[block], dq_r.at[plane], sem_dq, d * NX + dx, at(dy=d, dx=dx)))
        return copies

    def last_copy(d):
        block = rows(lax.rem(y + d, NY), base=FULL)
        return push(dq_s.at[block], dl_r.at[y], sem_dq, NY * NX + d, at(dy=d))

    def query_step(i, _):
        span, keys = spans(i)
        dot = dot_r[0, :, span]
        for j in range(1, NY):
            dot = dot + dot_r[j, :, span]
        ds = (wide(probs[:, span]) * (wide(gp[:, span]) - dot)).astype(BF)
        gp[:, span] = ds
        dq_s[span, :] = (FACTOR * mm(ds, k_all[keys, :], TN)).astype(BF)
        return 0

    for d in (2, 1, 3, 0):
        first = lax.rem(y + d, NY) * 2
        lax.fori_loop(first, first + 2, query_step, 0)
        start(query_copies(d))
    lax.fori_loop(FULL_CHUNKS, CHUNKS, query_step, 0)
    to_dl = [last_copy(d) for d in range(1, NY)]
    start(to_dl)
    dq_r[plane] = dq_s[rows(plane), :]
    dl_r[y] = dq_s[rows(y, base=FULL), :]
    key_sums(gp, q_all, dk_s, dk_r, sem_dk, FACTOR)
    to_dk = all_key_copies(dk_s, dk_r, sem_dk)
    to_wz.wait_recv()
    start([to_w[1]] + on_x)
    arrived([to_w[0], to_w[2]])
    start([on_z[0], on_z[2]])
    to_dq = [copy for d in range(NY) for copy in query_copies(d)]

    def key_total(part_index, got):
        for h in range(NX):
            total = wide(got[h * NZ, 0])
            for j in range(1, NZ):
                total = total + wide(got[h * NZ + j, 0])
            a_all[part_index, rows(y), h * HEAD_DIM : (h + 1) * HEAD_DIM] = total.astype(BF)
        total = wide(got[0, 1])
        for j in range(1, NK):
            total = total + wide(got[j, 1])
        a_all[part_index, rows(y), NX * HEAD_DIM :] = total.astype(BF)

    def a_copies(k):
        mine = a_all.at[k, rows(y)]
        return [push(mine, mine, sem_a, k * NY + d, at(dy=d)) for d in range(1, NY)]

    to_a = [a_copies(k) for k in range(3)]
    arrived(to_dv)
    key_total(2, dv_r)
    start(to_a[2])
    arrived(to_dq + to_dl)
    for h in range(NX):
        total = wide(dq_r[h])
        for j in range(1, NY):
            total = total + wide(dq_r[j * NX + h])
        a_all[0, rows(y), h * HEAD_DIM : (h + 1) * HEAD_DIM] = total.astype(BF)
    total = wide(dl_r[0])
    for j in range(1, NY):
        total = total + wide(dl_r[j])
    a_all[0, rows(y), NX * HEAD_DIM :] = total.astype(BF)
    start(to_a[0])
    arrived([to_w[1]])
    start([on_z[1]])
    arrived(to_dk)
    key_total(1, dk_r)
    start(to_a[1])
    arrived(on_x + on_z)
    for k in (2, 0, 1):
        arrived(to_a[k])

    def project(first, size):
        span = pl.ds(pl.multiple_of(first, HEAD_DIM), size)
        total = mm(a_all[0], w_all[0, span, :], NT)
        total = total + mm(a_all[1], w_all[1, span, :], NT)
        return total + mm(a_all[2], w_all[2, span, :], NT)

    to_c = []
    for n, (first, size) in enumerate(PIECES):
        part[:, first : first + size] = project((1 - core) * HALF + first, size).astype(BF)
        span = pl.ds(first, size)
        copy = push(part.at[:, span], pair.at[:, span], sem_c, n, partner)
        copy.start()
        to_c.append(copy)

    def out_copy(n, d):
        first, size = PIECES[n]
        to = lax.rem(y + d, NY)
        span = pl.ds(pl.multiple_of(core * HALF + first, HEAD_DIM), size)
        return push(
            pair.at[rows(to), pl.ds(first, size)], red.at[zl, :, span], sem_o, n * NY + d,
            (y // 2, lax.rem(y, 2), to, x, zh), n * NY + c,
        )

    for n, (first, size) in enumerate(PIECES):
        total = project(core * HALF + first, size)
        to_c[n].wait_recv()
        span = pl.ds(first, size)
        pair[:, span] = (total + wide(pair[:, span])).astype(BF)
        for d in (2, 1, 3):
            out_copy(n, d).start()

        @pl.when(c == y)
        def _():
            red[zl, :, pl.ds(pl.multiple_of(core * HALF + first, HEAD_DIM), size)] = pair[rows(y), span]

        @pl.when(c != y)
        def _():
            out_copy(n, 0).start()

    for n, (first, size) in enumerate(PIECES):
        for other in range(TY):
            @pl.when((c != y) | (c != other))
            def _():
                push(
                    pair.at[rows(0), pl.ds(first, size)], red.at[other // 2, :, pl.ds((other % 2) * HALF + first, size)],
                    sem_o, n * NY, at(dy=1), n * NY + other,
                ).wait_recv()
        for half in range(2):
            span = pl.ds(half * HALF + first, size)
            out[:, span] = (wide(red[0, :, span]) + wide(red[1, :, span])).astype(BF)

    done = to_p + on_p + [to_wz] + to_k + to_q + to_v + to_w + on_x + on_z + to_g + to_st + to_rd + to_dv + to_dq + to_dl + to_dk
    for copy in done + to_a[0] + to_a[1] + to_a[2] + to_c:
        copy.wait_send()
    halo_wait(f_made, f_got, sem_hf, sent=True)
    halo_wait(m_made, m_got, sem_hm, sent=True)
    for n in range(len(PIECES)):
        for d in range(1, NY):
            out_copy(n, d).wait_send()

        @pl.when(c != y)
        def _():
            out_copy(n, 0).wait_send()


def body(
    out_grad,
    preact,
    norm_gain,
    mid_weight,
    up_weight,
    patch_weight,
    query_proj,
    key_proj,
    value_proj,
    qkv_weight,
):
    any_space = pl.BlockSpec(memory_space=pl.ANY)

    def sems(count):
        return pltpu.SemaphoreType.DMA((2, count))

    in_vmem = pl.BlockSpec(memory_space=pltpu.VMEM)

    def strips(count, *shape):
        return pltpu.VMEM((count, 2) + shape, F32)

    return pl.pallas_call(
        whole_kernel,
        out_shape=(
            jax.ShapeDtypeStruct((2, 16, 8, CH), BF),
            jax.ShapeDtypeStruct((TOK, OUT), BF),
        ),
        in_specs=[any_space] + [in_vmem] * 2 + [any_space] * 7,
        out_specs=(in_vmem, in_vmem),
        scratch_shapes=[
            pltpu.VMEM((2, 16, 2, 16, FINE), BF),
            pltpu.VMEM((2, 2, 17, 2, 32, HEAD_DIM), F32),
            pltpu.VMEM((3, 2, 17, 2, 8, FINE), F32),
            pltpu.VMEM((2, 9, FINE, CH), BF),
            pltpu.VMEM((2, 9, CH, CH), BF),
            pltpu.VMEM((2, 18, 24, CH), F32),
            pltpu.VMEM((3, 2, 16, 8, HEAD_DIM), F32),
            pltpu.VMEM((32, PATCH), F32),
            strips(2, 16, FINE),
            strips(2, 16, 2, 1, FINE),
            strips(4, 1, FINE),
            strips(2, 16, FINE),
            strips(2, 16, 2, 1, FINE),
            strips(4, 1, FINE),
            strips(2, 8, CH),
            strips(2, 16, 1, CH),
            strips(4, 1, CH),
            strips(2, 8, CH),
            strips(2, 16, 1, CH),
            strips(4, 1, CH),
            sems(8),
            sems(8),
            pltpu.VMEM((TOK, PATCH), BF),
            pltpu.VMEM((PATCH, COLS), BF),
            pltpu.VMEM((QUERIES, HEAD_DIM), BF),
            pltpu.VMEM((2 * KEYS, HEAD_DIM), BF),
            pltpu.VMEM((2 * KEYS, HEAD_DIM), BF),
            pltpu.VMEM((TOK, COLS), BF),
            pltpu.VMEM((QUERIES, HEAD_DIM), BF),
            pltpu.VMEM((3, OUT, COLS), BF),
            pltpu.VMEM((KEYS, QUERIES), BF),
            pltpu.VMEM((KEYS, QUERIES), BF),
            pltpu.VMEM((2, 1, QUERIES), F32),
            pltpu.VMEM((NY, 2, 1, QUERIES), F32),
            pltpu.VMEM((1, QUERIES), F32),
            pltpu.VMEM((NY, 1, QUERIES), F32),
            pltpu.VMEM((QUERIES, HEAD_DIM), BF),
            pltpu.VMEM((NY * NX, TOK, HEAD_DIM), BF),
            pltpu.VMEM((NY, TOK, HEAD_DIM), BF),
            pltpu.VMEM((2, KEYS, HEAD_DIM), BF),
            pltpu.VMEM((NK, 2, TOK, HEAD_DIM), BF),
            pltpu.VMEM((2, KEYS, HEAD_DIM), BF),
            pltpu.VMEM((NK, 2, TOK, HEAD_DIM), BF),
            pltpu.VMEM((3, LAST, COLS), BF),
            pltpu.VMEM((LAST, HALF), BF),
            pltpu.VMEM((LAST, HALF), BF),
            pltpu.VMEM((2, TOK, OUT), BF),
            sems(TY),
            sems(NY * NX + NY),
            sems(2 * NK),
            sems(2 * NK),
            sems(3 * NX),
            sems(NY * NX + NY),
            sems(NY),
            sems(NY),
            sems(NY * NX + NY),
            sems(2 * NK),
            sems(2 * NK),
            sems(3 * NY),
            sems(len(PIECES)),
            sems(len(PIECES) * NY),
            pltpu.SemaphoreType.DMA((11,)),
        ],
        compiler_params=pltpu.CompilerParams(
            collective_id=0, has_side_effects=True, vmem_limit_bytes=56 * 1024 * 1024
        ),
        name="whole",
    )(
        out_grad.reshape(2, 16, 2, 16, FINE),
        preact,
        norm_gain,
        up_weight.transpose(0, 1, 2, 4, 3).reshape(3, 9, FINE, CH),
        mid_weight.reshape(3, 9, CH, CH),
        patch_weight,
        query_proj,
        key_proj,
        value_proj,
        qkv_weight.transpose(1, 0, 2),
    )


def solution(mesh):
    split = Mesh(mesh.devices.reshape(SIZES), AXES)
    ty, tx = ("zl", "core"), ("y", "x", "zh")
    placed = (
        P(None, ty, tx, None),
        P(None, ty, tx, None),
        P(),
        P(),
        P(),
        P(None, ty),
        P(tx, ty),
        P(tx, ty),
        P(tx, ty),
        P(tx, None, ty),
    )
    return jax.shard_map(
        body,
        mesh=split,
        in_specs=placed,
        out_specs=(P(None, ty, tx, None), P(tx, ty)),
        check_vma=False,
    )
```

```python
import jax
import jax.numpy as jnp
from jax import lax
from jax.experimental import pallas as pl
from jax.experimental.pallas import tpu as pltpu
from jax.sharding import Mesh
from jax.sharding import PartitionSpec as P

HEAD_DIM = 128

BF = jnp.bfloat16
F32 = jnp.float32
MESH = pl.DeviceIdType.MESH
NN = (((1,), (0,)), ((), ()))
NT = (((1,), (1,)), ((), ()))
TN = (((0,), (0,)), ((), ()))
AXES = ("zl", "core", "y", "x", "zh")
SIZES = (2, 2, 4, 4, 2)
NX, NY, NZ, TY = 4, 4, 2, 4
NK = NX * NZ
HEADS, TOK, COLS = 5, 128, 640
FULL = NX * NY * TOK
LAST = NY * TOK
QUERIES = FULL + LAST
KEYS = NK * TOK
CHUNK = 256
FULL_CHUNKS = FULL // CHUNK
CHUNKS = QUERIES // CHUNK
ROWS_W = 160
CUT_W = 64
EARLY_W = 64
OUT = NK * ROWS_W
HALF = OUT // 2
PIECES = ((0, 256), (256, 256), (512, 128))
PATCH = 3072
FACTOR = HEAD_DIM ** (-0.5)
LOG2E = 1.4426950408889634


CH, FINE = 384, 192
AROUND = ((-1, 0), (1, 0), (0, -1), (0, 1), (-1, -1), (-1, 1), (1, -1), (1, 1))
ACROSS = (1, 0, 3, 2, 7, 6, 5, 4)
COLUMNS = NY * NX * NZ


def mm(one, two, dims=NN):
    return lax.dot_general(one, two, dims, preferred_element_type=F32)


def wide(tile):
    return tile.astype(F32)


def whole_kernel(
    fine, preact, gain, up_w, mid_w, patch_w, query, key, value, weight, feature, out,
    g_in, gf, vf, uw, mw, mf, ff, ps, fs_row, fs_col, fs_cor, fr_row, fr_col, fr_cor,
    ms_row, ms_col, ms_cor, mr_row, mr_col, mr_cor, sem_hf, sem_hm,
    p_all, pw, q_all, k_all, v_all, g_own, g_all, w_all, probs, gp, stat_s, stat_r, dot_s, dot_r,
    dq_s, dq_r, dl_r, dk_s, dk_r, dv_s, dv_r, a_all, part, pair, red,
    sem_p, sem_q, sem_k, sem_v, sem_w, sem_g, sem_st, sem_rd, sem_dq, sem_dk, sem_dv, sem_a, sem_c, sem_o, sem_l,
):
    zl, core, y, x, zh = [lax.axis_index(name) for name in AXES]
    c = zl * 2 + core

    def at(dty=0, dy=0, dx=0, dz=0):
        ty = lax.rem(c + dty, TY)
        return (ty // 2, lax.rem(ty, 2), lax.rem(y + dy, NY), lax.rem(x + dx, NX), lax.rem(zh + dz, NZ))

    partner = (zl, 1 - core, y, x, zh)

    def rows(index, size=TOK, base=0):
        return pl.ds(pl.multiple_of(index * size + base, 32), size)

    def cols(h):
        return pl.ds(pl.multiple_of(h * HEAD_DIM, HEAD_DIM), HEAD_DIM)

    def push(src, dst, sems, index, target, arrives=None):
        return pltpu.make_async_remote_copy(
            src_ref=src, dst_ref=dst, send_sem=sems.at[0, index],
            recv_sem=sems.at[1, index if arrives is None else arrives],
            device_id=target, device_id_type=MESH,
        )

    def start(copies):
        for copy in copies:
            copy.start()

    def arrived(copies):
        for copy in copies:
            copy.wait_recv()

    greet = [at(dty=a, dy=b) for a in range(TY) for b in range(NY) if a or b]
    greet += [at(dy=a, dx=b) for a in range(NY) for b in range(1, NX)]
    greet += [at(dx=a, dz=1) for a in range(NX)]
    place = (y * NX + x) * NZ + zh

    def neighbour(i):
        ty = lax.rem(c + AROUND[i][0] + TY, TY)
        t = lax.rem(place + AROUND[i][1] + COLUMNS, COLUMNS)
        return (ty // 2, lax.rem(ty, 2), t // NK, lax.rem(t // NZ, NX), lax.rem(t, NZ))

    def exists(i):
        ty, t = c + AROUND[i][0], place + AROUND[i][1]
        return (ty >= 0) & (ty < TY) & (t >= 0) & (t < COLUMNS)

    def halo_start(made, got, sems):
        for i in range(8):
            @pl.when(exists(i))
            def _():
                push(made[i], got[ACROSS[i]], sems, i, neighbour(i), ACROSS[i]).start()

            @pl.when(jnp.logical_not(exists(i)))
            def _():
                got[i][...] = jnp.zeros(got[i].shape, F32)

    def halo_wait(made, got, sems, sent=False):
        for i in range(8):
            @pl.when(exists(i))
            def _():
                copy = push(made[i], got[i], sems, i, neighbour(i), i)
                if sent:
                    copy.wait_send()
                else:
                    copy.wait_recv()

    greet += [neighbour(i) for i in range(2, 8)]
    barrier = pltpu.get_barrier_semaphore()
    for other in greet:
        pl.semaphore_signal(barrier, inc=1, device_id=other, device_id_type=MESH)

    plane = y * NX + x
    line = x * NZ + zh
    def load(src, dst, index):
        return pltpu.make_async_copy(src, dst, sem_l.at[index])

    in_fine = load(fine, g_in, 0)
    in_up = load(up_w.at[pl.ds(1, 2)], uw, 1)
    in_mid = load(mid_w.at[pl.ds(1, 2)], mw, 2)
    in_patch = load(patch_w, pw, 3)
    in_weight = load(weight, w_all.at[:, rows(line, ROWS_W)], 4)
    in_key = [
        load(key.at[:, cols(x)], k_all.at[rows(line)], 5),
        load(key.at[:, cols(NX)], k_all.at[rows(line, base=KEYS)], 6),
    ]
    in_rest = [
        load(value.at[:, cols(x)], v_all.at[rows(line)], 7),
        load(value.at[:, cols(NX)], v_all.at[rows(line, base=KEYS)], 8),
        load(query.at[:, cols(x)], q_all.at[rows(plane)], 9),
        load(query.at[:, cols(NX)], q_all.at[rows(y, base=FULL)], 10),
    ]
    start([in_fine] + in_key + [in_up] + in_rest + [in_mid, in_patch, in_weight])

    in_fine.wait()
    lanes = ((0, 0, HEAD_DIM), (1, HEAD_DIM, FINE - HEAD_DIM))
    for k, first, size in lanes:
        span = slice(first, first + size)
        gf[k, :, 0:16, 1, 8:24, :size] = wide(g_in[:, :, 0, :, span])
        gf[k, :, 1:17, 0, 8:24, :size] = wide(g_in[:, :, 1, :, span])
        for side, col in ((0, 8), (1, 23)):
            fs_col[side, :, :, 0, :, span] = gf[k, :, 0:16, 1, col : col + 1, :size]
            fs_col[side, :, :, 1, :, span] = gf[k, :, 1:17, 0, col : col + 1, :size]
            fs_cor[side, :, :, span] = gf[k, :, 0, 1, col : col + 1, :size]
            fs_cor[2 + side, :, :, span] = gf[k, :, 16, 0, col : col + 1, :size]
    fs_row[0] = wide(g_in[:, 0, 0])
    fs_row[1] = wide(g_in[:, 15, 1])
    pl.semaphore_wait(barrier, len(greet))
    f_made = [fs_row.at[0], fs_row.at[1], fs_col.at[0], fs_col.at[1]] + [fs_cor.at[i] for i in range(4)]
    f_got = [fr_row.at[0], fr_row.at[1], fr_col.at[0], fr_col.at[1]] + [fr_cor.at[i] for i in range(4)]
    halo_start(f_made, f_got, sem_hf)

    def to_queries(src, dst, sems):
        copies = []
        for dy in range(NY):
            for dx in range(NX):
                if dy or dx:
                    head = cols(lax.rem(x + dx, NX))
                    copies.append(push(src.at[:, head], dst.at[rows(plane)], sems, dy * NX + dx, at(dy=dy, dx=dx)))
            if dy:
                copies.append(push(src.at[:, cols(NX)], dst.at[rows(y, base=FULL)], sems, NY * NX + dy, at(dy=dy)))
        return copies

    def keys_over_x(src, dst, sems):
        copies = []
        for d in range(1, NX):
            head = cols(lax.rem(x + d, NX))
            copies.append(push(src.at[:, head], dst.at[rows(line)], sems, 2 * d, at(dx=d)))
            copies.append(push(src.at[:, cols(NX)], dst.at[rows(line, base=KEYS)], sems, 2 * d + 1, at(dx=d)))
        return copies

    def keys_over_z(dst, sems, steps):
        copies = []
        for d in steps:
            block = lax.rem(x - d + NX, NX) * NZ + zh
            for k in range(2):
                there = dst.at[rows(block, base=k * KEYS)]
                copies.append(push(there, there, sems, 2 * NX + 2 * d + k, at(dz=1)))
        return copies

    own_p = p_all.at[rows(c, 32)]
    over_z = lax.rem(c + 2, TY)
    far_p = p_all.at[rows(over_z, 32)]
    to_p = [push(own_p, own_p, sem_p, 0, at(dty=2)), push(own_p, own_p, sem_p, 1, partner)]
    on_p = [push(far_p, far_p, sem_p, 2, partner)]
    kx, vx = keys_over_x(key, k_all, sem_k), keys_over_x(value, v_all, sem_v)
    kz, vz = keys_over_z(k_all, sem_k, (1, 2, 3)), keys_over_z(v_all, sem_v, (1, 2, 3))
    own_kz, own_vz = keys_over_z(k_all, sem_k, (0,)), keys_over_z(v_all, sem_v, (0,))
    to_k, to_v = kx + kz + own_kz, vx + vz + own_vz
    to_q = to_queries(query, q_all, sem_q)

    def some_rows(d, first, size, slot):
        mine = w_all.at[:, pl.ds(pl.multiple_of(line * ROWS_W + first, 16), size)]
        return push(weight.at[:, pl.ds(first, size)], mine, sem_w, slot + d, at(dx=d))

    wx = [
        [some_rows(d, 0, EARLY_W, 0) for d in range(1, NX)],
        [some_rows(d, EARLY_W, ROWS_W - EARLY_W, 3 * NX) for d in range(1, NX)],
    ]
    wz = [
        push(weight.at[:, pl.ds(first, size)], w_all.at[:, pl.ds(pl.multiple_of(line * ROWS_W + first, 16), size)], sem_w, slot, at(dz=1))
        for first, size, slot in ((0, CUT_W, 0), (CUT_W, ROWS_W - CUT_W, 3 * NX))
    ]
    for copy in in_key:
        copy.wait()
    start(kx + own_kz + wz[:1])
    beside = w_all.at[:, pl.ds(pl.multiple_of((x * NZ + 1 - zh) * ROWS_W, 16), CUT_W)]
    on_x = [push(beside, beside, sem_w, NX + d, at(dx=d)) for d in range(1, NX)]
    on_z = []
    for d in range(1, NX):
        first = lax.rem(x - d + NX, NX) * NZ + zh
        below = w_all.at[:, pl.ds(pl.multiple_of(first * ROWS_W + CUT_W, 16), ROWS_W - CUT_W)]
        on_z.append(push(below, below, sem_w, 2 * NX + d, at(dz=1)))

    halo_wait(f_made, f_got, sem_hf)
    for k, first, size in lanes:
        span = slice(first, first + size)
        gf[k, :, 0, 0, 8:24, :size] = fr_row[0, :, :, span]
        gf[k, :, 16, 1, 8:24, :size] = fr_row[1, :, :, span]
        for side, col in ((0, 7), (1, 24)):
            gf[k, :, 0:16, 1, col : col + 1, :size] = fr_col[side, :, :, 0, :, span]
            gf[k, :, 1:17, 0, col : col + 1, :size] = fr_col[side, :, :, 1, :, span]
            gf[k, :, 0, 0, col : col + 1, :size] = fr_cor[side, :, :, span]
            gf[k, :, 16, 1, col : col + 1, :size] = fr_cor[2 + side, :, :, span]
        for f in range(2):
            four = [gf[k, f, :, :, pl.ds(7 + s, 8, stride=2), :][..., :size] for s in range(4)]
            for tap in range(3):
                vf[tap, f, :, :, :, span] = four[2 - tap] + four[3 - tap]
    in_up.wait()

    def causal(cells, weights, dims):
        own = later = None
        for tap in range(9):
            both = jnp.concatenate([cells(0, tap), cells(1, tap)], axis=0)
            one = mm(both, weights[1, tap], dims)
            two = mm(both[TOK:], weights[0, tap], dims)
            own = one if own is None else own + one
            later = two if later is None else later + two
        return own[:TOK] + later, own[TOK:]

    def fine_cells(f, tap):
        b, col = tap // 3, tap % 3
        one = vf[col, f, 0:16, 1] if b else vf[col, f, 1:17, 0]
        two = (vf[col, f, 1:17, 1], vf[col, f, 1:17, 0], vf[col, f, 0:16, 0])[b]
        return (one + two).reshape(TOK, FINE).astype(BF)

    scale = gain[...].reshape(1, CH)
    for f, pooled in enumerate(causal(fine_cells, uw, NN)):
        z = scale * wide(preact[f].reshape(TOK, CH))
        s = 1.0 / (1.0 + jnp.exp(-z))
        mid = (pooled * scale * s * (1.0 + z * (1.0 - s))).astype(BF)
        mf[f, 1:17, 8:16, :] = wide(mid).reshape(16, 8, CH)
    ms_row[0] = mf[:, 1, 8:16, :]
    ms_row[1] = mf[:, 16, 8:16, :]
    for side, col in ((0, 8), (1, 15)):
        ms_col[side] = mf[:, 1:17, col : col + 1, :]
        ms_cor[side] = mf[:, 1, col : col + 1, :]
        ms_cor[2 + side] = mf[:, 16, col : col + 1, :]
    m_made = [ms_row.at[0], ms_row.at[1], ms_col.at[0], ms_col.at[1]] + [ms_cor.at[i] for i in range(4)]
    m_got = [mr_row.at[0], mr_row.at[1], mr_col.at[0], mr_col.at[1]] + [mr_cor.at[i] for i in range(4)]
    halo_start(m_made, m_got, sem_hm)
    arrived(kx)
    start(kz + to_q + vx + [wx[0][0], wx[0][2]])
    in_mid.wait()
    halo_wait(m_made, m_got, sem_hm)
    mf[:, 0, 8:16, :] = mr_row[0]
    mf[:, 17, 8:16, :] = mr_row[1]
    for side, col in ((0, 7), (1, 16)):
        mf[:, 1:17, col : col + 1, :] = mr_col[side]
        mf[:, 0, col : col + 1, :] = mr_cor[side]
        mf[:, 17, col : col + 1, :] = mr_cor[2 + side]

    def mid_cells(f, tap):
        b, col = tap // 3, tap % 3
        return mf[f, 2 - b : 18 - b, 9 - col : 17 - col, :].reshape(TOK, CH).astype(BF)

    for f, total in enumerate(causal(mid_cells, mw, NT)):
        low = total.astype(BF)
        feature[f] = low.reshape(16, 8, CH)
        for k in range(3):
            ff[k, f] = wide(low[:, k * HEAD_DIM : (k + 1) * HEAD_DIM]).reshape(16, 8, HEAD_DIM)
    for t in range(2):
        for u in range(2):
            for w in range(2):
                first = ((t * 2 + u) * 2 + w) * CH
                for k in range(3):
                    span = slice(first + k * HEAD_DIM, first + (k + 1) * HEAD_DIM)
                    for p in range(8):
                        ps[p * 4 : p * 4 + 4, span] = ff[k, t, 2 * p + u, pl.ds(w, 4, stride=2), :]
    p_all[rows(c, 32), :] = ps[...].astype(BF)
    start(to_p)

    arrived(to_p[:1])
    start(on_p)
    for copy in in_rest + [in_patch, in_weight]:
        copy.wait()
    arrived(vx)
    start(own_vz + vz + wz[1:])
    arrived(to_p[1:] + on_p)
    g_own[...] = mm(p_all[...], pw[...]).astype(BF)
    to_g = to_queries(g_own, g_all, sem_g)
    start(to_g)
    start([wx[1][0], wx[1][2]])
    g_all[rows(plane), :] = g_own[:, cols(x)]
    g_all[rows(y, base=FULL), :] = g_own[:, cols(NX)]

    arrived(kz + own_kz + to_q)

    def spans(i):
        return rows(i, CHUNK), rows(i // FULL_CHUNKS, KEYS)

    def score_step(i, _):
        span, keys = spans(i)
        s = mm(k_all[keys, :], q_all[span, :], NT) * (FACTOR * LOG2E)
        peak = jnp.max(s, axis=0, keepdims=True)
        e = jnp.exp2(s - peak)
        stat_s[0, :, span] = peak
        stat_s[1, :, span] = jnp.sum(e, axis=0, keepdims=True)
        probs[:, span] = e.astype(BF)
        return 0

    lax.fori_loop(0, CHUNKS, score_step, 0, unroll=2)
    to_st = [push(stat_s, stat_r.at[y], sem_st, d, at(dy=d)) for d in range(1, NY)]
    start(to_st)
    stat_r[y] = stat_s[...]
    arrived(to_st)

    def share_step(i, _):
        span, _ = spans(i)
        top = stat_r[0, 0, :, span]
        for j in range(1, NY):
            top = jnp.maximum(top, stat_r[j, 0, :, span])
        total = jnp.zeros_like(top)
        for j in range(NY):
            total = total + stat_r[j, 1, :, span] * jnp.exp2(stat_r[j, 0, :, span] - top)
        share = jnp.exp2(stat_s[0, :, span] - top) / total
        probs[:, span] = (wide(probs[:, span]) * share).astype(BF)
        return 0

    lax.fori_loop(0, CHUNKS, share_step, 0, unroll=2)
    arrived(vz + own_vz + to_g)

    def grad_step(i, _):
        span, keys = spans(i)
        g = mm(v_all[keys, :], g_all[span, :], NT)
        dot_s[:, span] = jnp.sum(wide(probs[:, span]) * g, axis=0, keepdims=True)
        gp[:, span] = g.astype(BF)
        return 0

    lax.fori_loop(0, CHUNKS, grad_step, 0, unroll=2)
    to_rd = [push(dot_s, dot_r.at[y], sem_rd, d, at(dy=d)) for d in range(1, NY)]
    start(to_rd)
    dot_r[y] = dot_s[...]

    def key_copies(d, made, got, sems):
        copies = []
        block = lax.rem(x + d, NX) * NZ
        for dz in range(NZ):
            if d or dz:
                there = block + lax.rem(zh + dz, NZ)
                for k in range(2):
                    copies.append(
                        push(made.at[k, rows(there)], got.at[line, k], sems, 2 * (d * NZ + dz) + k, at(dx=d, dz=dz))
                    )
        return copies

    def key_sums(left, right, made, got, sems, scale):
        for d in (2, 1, 3, 0):
            block = rows(lax.rem(x + d, NX), NZ * TOK)
            made[0, block, :] = (scale * mm(left[block, :FULL], right[:FULL, :])).astype(BF)
            made[1, block, :] = (scale * mm(left[block, FULL:], right[FULL:, :])).astype(BF)
            start(key_copies(d, made, got, sems))
        got[line] = made[:, rows(line), :]

    def all_key_copies(made, got, sems):
        return [copy for d in range(NX) for copy in key_copies(d, made, got, sems)]

    key_sums(probs, g_all, dv_s, dv_r, sem_dv, 1.0)
    to_dv = all_key_copies(dv_s, dv_r, sem_dv)
    arrived(to_rd)

    def query_copies(d):
        copies = []
        there = lax.rem(y + d, NY)
        for dx in range(NX):
            if d or dx:
                block = rows(there * NX + lax.rem(x + dx, NX))
                copies.append(push(dq_s.at[block], dq_r.at[plane], sem_dq, d * NX + dx, at(dy=d, dx=dx)))
        return copies

    def last_copy(d):
        block = rows(lax.rem(y + d, NY), base=FULL)
        return push(dq_s.at[block], dl_r.at[y], sem_dq, NY * NX + d, at(dy=d))

    def query_step(i, _):
        span, keys = spans(i)
        dot = dot_r[0, :, span]
        for j in range(1, NY):
            dot = dot + dot_r[j, :, span]
        ds = (wide(probs[:, span]) * (wide(gp[:, span]) - dot)).astype(BF)
        gp[:, span] = ds
        dq_s[span, :] = (FACTOR * mm(ds, k_all[keys, :], TN)).astype(BF)
        return 0

    for d in (2, 1, 3, 0):
        first = lax.rem(y + d, NY) * 2
        query_step(first, 0)
        query_step(first + 1, 0)
        start(query_copies(d))
    query_step(FULL_CHUNKS, 0)
    query_step(FULL_CHUNKS + 1, 0)
    to_dl = [last_copy(d) for d in range(1, NY)]
    start(to_dl)
    dq_r[plane] = dq_s[rows(plane), :]
    dl_r[y] = dq_s[rows(y, base=FULL), :]
    key_sums(gp, q_all, dk_s, dk_r, sem_dk, FACTOR)
    to_dk = all_key_copies(dk_s, dk_r, sem_dk)
    arrived(wz[:1])
    start([wx[0][1], wx[1][1]] + on_x)
    to_dq = [copy for d in range(NY) for copy in query_copies(d)]

    def key_total(part_index, got):
        for h in range(NX):
            total = wide(got[h * NZ, 0])
            for j in range(1, NZ):
                total = total + wide(got[h * NZ + j, 0])
            a_all[part_index, rows(y), h * HEAD_DIM : (h + 1) * HEAD_DIM] = total.astype(BF)
        total = wide(got[0, 1])
        for j in range(1, NK):
            total = total + wide(got[j, 1])
        a_all[part_index, rows(y), NX * HEAD_DIM :] = total.astype(BF)

    def a_copies(k):
        mine = a_all.at[k, rows(y)]
        return [push(mine, mine, sem_a, k * NY + d, at(dy=d)) for d in (1, 3)]

    def a_onward(k):
        half = TOK // 2
        up = a_all.at[k, pl.ds(pl.multiple_of(lax.rem(y + 3, NY) * TOK, half), half)]
        down = a_all.at[k, pl.ds(pl.multiple_of(lax.rem(y + 1, NY) * TOK + half, half), half)]
        return [push(up, up, sem_a, k * NY, at(dy=1)), push(down, down, sem_a, k * NY + 2, at(dy=3))]

    to_a = [a_copies(k) for k in range(3)]
    on_a = [a_onward(k) for k in range(3)]
    arrived(to_dv)
    key_total(2, dv_r)
    start(to_a[2])
    arrived([wx[0][0], wx[0][2], wx[1][0], wx[1][2]])
    start([on_z[0], on_z[2]])
    arrived(to_dq + to_dl)
    for h in range(NX):
        total = wide(dq_r[h])
        for j in range(1, NY):
            total = total + wide(dq_r[j * NX + h])
        a_all[0, rows(y), h * HEAD_DIM : (h + 1) * HEAD_DIM] = total.astype(BF)
    total = wide(dl_r[0])
    for j in range(1, NY):
        total = total + wide(dl_r[j])
    a_all[0, rows(y), NX * HEAD_DIM :] = total.astype(BF)
    start(to_a[0])
    arrived(to_a[2])
    start(on_a[2])
    arrived([wx[0][1], wx[1][1]])
    start([on_z[1]])
    arrived(to_dk)
    key_total(1, dk_r)
    start(to_a[1])
    arrived(to_a[0])
    start(on_a[0])
    arrived(to_a[1])
    start(on_a[1])
    for k in (2, 0, 1):
        arrived(on_a[k])
    arrived(wz[1:] + on_x + on_z)

    def project(first, size):
        span = pl.ds(pl.multiple_of(first, HEAD_DIM), size)
        total = mm(a_all[0], w_all[0, span, :], NT)
        total = total + mm(a_all[1], w_all[1, span, :], NT)
        return total + mm(a_all[2], w_all[2, span, :], NT)

    to_c = []
    for n, (first, size) in enumerate(PIECES):
        part[:, first : first + size] = project((1 - core) * HALF + first, size).astype(BF)
        span = pl.ds(first, size)
        copy = push(part.at[:, span], pair.at[:, span], sem_c, n, partner)
        copy.start()
        to_c.append(copy)

    def out_copy(n, d):
        first, size = PIECES[n]
        to = lax.rem(y + d, NY)
        span = pl.ds(pl.multiple_of(core * HALF + first, HEAD_DIM), size)
        return push(
            pair.at[rows(to), pl.ds(first, size)], red.at[zl, :, span], sem_o, n * NY + d,
            (y // 2, lax.rem(y, 2), to, x, zh), n * NY + c,
        )

    for n, (first, size) in enumerate(PIECES):
        total = project(core * HALF + first, size)
        to_c[n].wait_recv()
        span = pl.ds(first, size)
        pair[:, span] = (total + wide(pair[:, span])).astype(BF)
        for d in (2, 1, 3):
            out_copy(n, d).start()

        @pl.when(c == y)
        def _():
            red[zl, :, pl.ds(pl.multiple_of(core * HALF + first, HEAD_DIM), size)] = pair[rows(y), span]

        @pl.when(c != y)
        def _():
            out_copy(n, 0).start()

    done = to_p + on_p + wz + to_k + to_q + to_v + wx[0] + wx[1] + on_x + on_z + to_g + to_st + to_rd + to_dv + to_dq + to_dl + to_dk
    for copy in done + to_a[0] + to_a[1] + to_a[2] + on_a[0] + on_a[1] + on_a[2] + to_c:
        copy.wait_send()
    halo_wait(f_made, f_got, sem_hf, sent=True)
    halo_wait(m_made, m_got, sem_hm, sent=True)

    for n, (first, size) in enumerate(PIECES):
        for other in range(TY):
            @pl.when((c != y) | (c != other))
            def _():
                push(
                    pair.at[rows(0), pl.ds(first, size)], red.at[other // 2, :, pl.ds((other % 2) * HALF + first, size)],
                    sem_o, n * NY, at(dy=1), n * NY + other,
                ).wait_recv()
        for half in range(2):
            span = pl.ds(half * HALF + first, size)
            out[:, span] = (wide(red[0, :, span]) + wide(red[1, :, span])).astype(BF)

    for n in range(len(PIECES)):
        for d in range(1, NY):
            out_copy(n, d).wait_send()

        @pl.when(c != y)
        def _():
            out_copy(n, 0).wait_send()


def body(
    out_grad,
    preact,
    norm_gain,
    mid_weight,
    up_weight,
    patch_weight,
    query_proj,
    key_proj,
    value_proj,
    qkv_weight,
):
    any_space = pl.BlockSpec(memory_space=pl.ANY)

    def sems(count):
        return pltpu.SemaphoreType.DMA((2, count))

    in_vmem = pl.BlockSpec(memory_space=pltpu.VMEM)

    def strips(count, *shape):
        return pltpu.VMEM((count, 2) + shape, F32)

    return pl.pallas_call(
        whole_kernel,
        out_shape=(
            jax.ShapeDtypeStruct((2, 16, 8, CH), BF),
            jax.ShapeDtypeStruct((TOK, OUT), BF),
        ),
        in_specs=[any_space] + [in_vmem] * 2 + [any_space] * 7,
        out_specs=(in_vmem, in_vmem),
        scratch_shapes=[
            pltpu.VMEM((2, 16, 2, 16, FINE), BF),
            pltpu.VMEM((2, 2, 17, 2, 32, HEAD_DIM), F32),
            pltpu.VMEM((3, 2, 17, 2, 8, FINE), F32),
            pltpu.VMEM((2, 9, FINE, CH), BF),
            pltpu.VMEM((2, 9, CH, CH), BF),
            pltpu.VMEM((2, 18, 24, CH), F32),
            pltpu.VMEM((3, 2, 16, 8, HEAD_DIM), F32),
            pltpu.VMEM((32, PATCH), F32),
            strips(2, 16, FINE),
            strips(2, 16, 2, 1, FINE),
            strips(4, 1, FINE),
            strips(2, 16, FINE),
            strips(2, 16, 2, 1, FINE),
            strips(4, 1, FINE),
            strips(2, 8, CH),
            strips(2, 16, 1, CH),
            strips(4, 1, CH),
            strips(2, 8, CH),
            strips(2, 16, 1, CH),
            strips(4, 1, CH),
            sems(8),
            sems(8),
            pltpu.VMEM((TOK, PATCH), BF),
            pltpu.VMEM((PATCH, COLS), BF),
            pltpu.VMEM((QUERIES, HEAD_DIM), BF),
            pltpu.VMEM((2 * KEYS, HEAD_DIM), BF),
            pltpu.VMEM((2 * KEYS, HEAD_DIM), BF),
            pltpu.VMEM((TOK, COLS), BF),
            pltpu.VMEM((QUERIES, HEAD_DIM), BF),
            pltpu.VMEM((3, OUT, COLS), BF),
            pltpu.VMEM((KEYS, QUERIES), BF),
            pltpu.VMEM((KEYS, QUERIES), BF),
            pltpu.VMEM((2, 1, QUERIES), F32),
            pltpu.VMEM((NY, 2, 1, QUERIES), F32),
            pltpu.VMEM((1, QUERIES), F32),
            pltpu.VMEM((NY, 1, QUERIES), F32),
            pltpu.VMEM((QUERIES, HEAD_DIM), BF),
            pltpu.VMEM((NY * NX, TOK, HEAD_DIM), BF),
            pltpu.VMEM((NY, TOK, HEAD_DIM), BF),
            pltpu.VMEM((2, KEYS, HEAD_DIM), BF),
            pltpu.VMEM((NK, 2, TOK, HEAD_DIM), BF),
            pltpu.VMEM((2, KEYS, HEAD_DIM), BF),
            pltpu.VMEM((NK, 2, TOK, HEAD_DIM), BF),
            pltpu.VMEM((3, LAST, COLS), BF),
            pltpu.VMEM((LAST, HALF), BF),
            pltpu.VMEM((LAST, HALF), BF),
            pltpu.VMEM((2, TOK, OUT), BF),
            sems(TY),
            sems(NY * NX + NY),
            sems(2 * NK),
            sems(2 * NK),
            sems(4 * NX),
            sems(NY * NX + NY),
            sems(NY),
            sems(NY),
            sems(NY * NX + NY),
            sems(2 * NK),
            sems(2 * NK),
            sems(3 * NY),
            sems(len(PIECES)),
            sems(len(PIECES) * NY),
            pltpu.SemaphoreType.DMA((11,)),
        ],
        compiler_params=pltpu.CompilerParams(
            collective_id=0, has_side_effects=True, vmem_limit_bytes=56 * 1024 * 1024
        ),
        name="whole",
    )(
        out_grad.reshape(2, 16, 2, 16, FINE),
        preact,
        norm_gain,
        up_weight.transpose(0, 1, 2, 4, 3).reshape(3, 9, FINE, CH),
        mid_weight.reshape(3, 9, CH, CH),
        patch_weight,
        query_proj,
        key_proj,
        value_proj,
        qkv_weight.transpose(1, 0, 2),
    )


def solution(mesh):
    split = Mesh(mesh.devices.reshape(SIZES), AXES)
    ty, tx = ("zl", "core"), ("y", "x", "zh")
    placed = (
        P(None, ty, tx, None),
        P(None, ty, tx, None),
        P(),
        P(),
        P(),
        P(None, ty),
        P(tx, ty),
        P(tx, ty),
        P(tx, ty),
        P(tx, None, ty),
    )
    return jax.shard_map(
        body,
        mesh=split,
        in_specs=placed,
        out_specs=(P(None, ty, tx, None), P(tx, ty)),
        check_vma=False,
    )
```

```python
import jax
import jax.numpy as jnp
from jax import lax
from jax.experimental import pallas as pl
from jax.experimental.pallas import tpu as pltpu
from jax.sharding import Mesh
from jax.sharding import PartitionSpec as P

HEAD_DIM = 128

BF = jnp.bfloat16
F32 = jnp.float32
MESH = pl.DeviceIdType.MESH
NN = (((1,), (0,)), ((), ()))
NT = (((1,), (1,)), ((), ()))
TN = (((0,), (0,)), ((), ()))
AXES = ("zl", "core", "y", "x", "zh")
SIZES = (2, 2, 4, 4, 2)
NX, NY, NZ, TY = 4, 4, 2, 4
NK = NX * NZ
HEADS, TOK, COLS = 5, 128, 640
FULL = NX * NY * TOK
LAST = NY * TOK
QUERIES = FULL + LAST
KEYS = NK * TOK
CHUNK = 256
FULL_CHUNKS = FULL // CHUNK
CHUNKS = QUERIES // CHUNK
ROWS_W = 160
CUT_W = 64
EARLY_W = 64
OUT = NK * ROWS_W
HALF = OUT // 2
PIECES = ((0, 256), (256, 256), (512, 128))
PATCH = 3072
FACTOR = HEAD_DIM ** (-0.5)
LOG2E = 1.4426950408889634


CH, FINE = 384, 192
AROUND = ((-1, 0), (1, 0), (0, -1), (0, 1), (-1, -1), (-1, 1), (1, -1), (1, 1))
ACROSS = (1, 0, 3, 2, 7, 6, 5, 4)
COLUMNS = NY * NX * NZ


def mm(one, two, dims=NN):
    return lax.dot_general(one, two, dims, preferred_element_type=F32)


def wide(tile):
    return tile.astype(F32)


def whole_kernel(
    fine, preact, gain, up_w, mid_w, patch_w, query, key, value, weight, feature, out,
    g_in, gf, vf, uw, mw, mf, ff, ps, fs_row, fs_col, fs_cor, fr_row, fr_col, fr_cor,
    ms_row, ms_col, ms_cor, mr_row, mr_col, mr_cor, sem_hf, sem_hm,
    p_all, pw, q_all, k_all, v_all, g_own, g_all, w_all, probs, gp, stat_s, stat_r, dot_s, dot_r,
    dq_s, dq_r, dl_r, dk_s, dk_r, dv_s, dv_r, a_all, part, pair, red,
    sem_p, sem_q, sem_k, sem_v, sem_w, sem_g, sem_st, sem_rd, sem_dq, sem_dk, sem_dv, sem_a, sem_c, sem_o, sem_l,
):
    zl, core, y, x, zh = [lax.axis_index(name) for name in AXES]
    c = zl * 2 + core

    def at(dty=0, dy=0, dx=0, dz=0):
        ty = lax.rem(c + dty, TY)
        return (ty // 2, lax.rem(ty, 2), lax.rem(y + dy, NY), lax.rem(x + dx, NX), lax.rem(zh + dz, NZ))

    partner = (zl, 1 - core, y, x, zh)

    def rows(index, size=TOK, base=0):
        return pl.ds(pl.multiple_of(index * size + base, 32), size)

    def cols(h):
        return pl.ds(pl.multiple_of(h * HEAD_DIM, HEAD_DIM), HEAD_DIM)

    def push(src, dst, sems, index, target, arrives=None):
        return pltpu.make_async_remote_copy(
            src_ref=src, dst_ref=dst, send_sem=sems.at[0, index],
            recv_sem=sems.at[1, index if arrives is None else arrives],
            device_id=target, device_id_type=MESH,
        )

    def start(copies):
        for copy in copies:
            copy.start()

    def arrived(copies):
        for copy in copies:
            copy.wait_recv()

    greet = [at(dty=a, dy=b) for a in range(TY) for b in range(NY) if a or b]
    greet += [at(dy=a, dx=b) for a in range(NY) for b in range(1, NX)]
    greet += [at(dx=a, dz=1) for a in range(NX)]
    place = (y * NX + x) * NZ + zh

    def neighbour(i):
        ty = lax.rem(c + AROUND[i][0] + TY, TY)
        t = lax.rem(place + AROUND[i][1] + COLUMNS, COLUMNS)
        return (ty // 2, lax.rem(ty, 2), t // NK, lax.rem(t // NZ, NX), lax.rem(t, NZ))

    def exists(i):
        ty, t = c + AROUND[i][0], place + AROUND[i][1]
        return (ty >= 0) & (ty < TY) & (t >= 0) & (t < COLUMNS)

    def halo_start(made, got, sems):
        for i in range(8):
            @pl.when(exists(i))
            def _():
                push(made[i], got[ACROSS[i]], sems, i, neighbour(i), ACROSS[i]).start()

            @pl.when(jnp.logical_not(exists(i)))
            def _():
                got[i][...] = jnp.zeros(got[i].shape, F32)

    def halo_wait(made, got, sems, sent=False):
        for i in range(8):
            @pl.when(exists(i))
            def _():
                copy = push(made[i], got[i], sems, i, neighbour(i), i)
                if sent:
                    copy.wait_send()
                else:
                    copy.wait_recv()

    greet += [neighbour(i) for i in range(2, 8)]
    barrier = pltpu.get_barrier_semaphore()
    for other in greet:
        pl.semaphore_signal(barrier, inc=1, device_id=other, device_id_type=MESH)

    plane = y * NX + x
    line = x * NZ + zh
    def load(src, dst, index):
        return pltpu.make_async_copy(src, dst, sem_l.at[index])

    in_fine = load(fine, g_in, 0)
    in_up = load(up_w.at[pl.ds(1, 2)], uw, 1)
    in_mid = load(mid_w.at[pl.ds(1, 2)], mw, 2)
    in_patch = load(patch_w, pw, 3)
    in_weight = load(weight, w_all.at[:, rows(line, ROWS_W)], 4)
    in_key = [
        load(key.at[:, cols(x)], k_all.at[rows(line)], 5),
        load(key.at[:, cols(NX)], k_all.at[rows(line, base=KEYS)], 6),
    ]
    in_rest = [
        load(value.at[:, cols(x)], v_all.at[rows(line)], 7),
        load(value.at[:, cols(NX)], v_all.at[rows(line, base=KEYS)], 8),
        load(query.at[:, cols(x)], q_all.at[rows(plane)], 9),
        load(query.at[:, cols(NX)], q_all.at[rows(y, base=FULL)], 10),
    ]
    start([in_fine] + in_key + [in_up] + in_rest + [in_mid, in_patch, in_weight])

    in_fine.wait()
    lanes = ((0, 0, HEAD_DIM), (1, HEAD_DIM, FINE - HEAD_DIM))
    for k, first, size in lanes:
        span = slice(first, first + size)
        gf[k, :, 0:16, 1, 8:24, :size] = wide(g_in[:, :, 0, :, span])
        gf[k, :, 1:17, 0, 8:24, :size] = wide(g_in[:, :, 1, :, span])
        for side, col in ((0, 8), (1, 23)):
            fs_col[side, :, :, 0, :, span] = gf[k, :, 0:16, 1, col : col + 1, :size]
            fs_col[side, :, :, 1, :, span] = gf[k, :, 1:17, 0, col : col + 1, :size]
            fs_cor[side, :, :, span] = gf[k, :, 0, 1, col : col + 1, :size]
            fs_cor[2 + side, :, :, span] = gf[k, :, 16, 0, col : col + 1, :size]
    fs_row[0] = wide(g_in[:, 0, 0])
    fs_row[1] = wide(g_in[:, 15, 1])
    pl.semaphore_wait(barrier, len(greet))
    f_made = [fs_row.at[0], fs_row.at[1], fs_col.at[0], fs_col.at[1]] + [fs_cor.at[i] for i in range(4)]
    f_got = [fr_row.at[0], fr_row.at[1], fr_col.at[0], fr_col.at[1]] + [fr_cor.at[i] for i in range(4)]
    halo_start(f_made, f_got, sem_hf)

    def to_queries(src, dst, sems):
        copies = []
        for dy in range(NY):
            for dx in range(NX):
                if dy or dx:
                    head = cols(lax.rem(x + dx, NX))
                    copies.append(push(src.at[:, head], dst.at[rows(plane)], sems, dy * NX + dx, at(dy=dy, dx=dx)))
            if dy:
                copies.append(push(src.at[:, cols(NX)], dst.at[rows(y, base=FULL)], sems, NY * NX + dy, at(dy=dy)))
        return copies

    def keys_over_x(src, dst, sems):
        copies = []
        for d in range(1, NX):
            head = cols(lax.rem(x + d, NX))
            copies.append(push(src.at[:, head], dst.at[rows(line)], sems, 2 * d, at(dx=d)))
            copies.append(push(src.at[:, cols(NX)], dst.at[rows(line, base=KEYS)], sems, 2 * d + 1, at(dx=d)))
        return copies

    def keys_over_z(dst, sems, steps):
        copies = []
        for d in steps:
            block = lax.rem(x - d + NX, NX) * NZ + zh
            for k in range(2):
                there = dst.at[rows(block, base=k * KEYS)]
                copies.append(push(there, there, sems, 2 * NX + 2 * d + k, at(dz=1)))
        return copies

    own_p = p_all.at[rows(c, 32)]
    over_z = lax.rem(c + 2, TY)
    far_p = p_all.at[rows(over_z, 32)]
    to_p = [push(own_p, own_p, sem_p, 0, at(dty=2)), push(own_p, own_p, sem_p, 1, partner)]
    on_p = [push(far_p, far_p, sem_p, 2, partner)]
    kx, vx = keys_over_x(key, k_all, sem_k), keys_over_x(value, v_all, sem_v)
    kz, vz = keys_over_z(k_all, sem_k, (1, 2, 3)), keys_over_z(v_all, sem_v, (1, 2, 3))
    own_kz, own_vz = keys_over_z(k_all, sem_k, (0,)), keys_over_z(v_all, sem_v, (0,))
    to_k, to_v = kx + kz + own_kz, vx + vz + own_vz
    to_q = to_queries(query, q_all, sem_q)

    def some_rows(d, first, size, slot):
        mine = w_all.at[:, pl.ds(pl.multiple_of(line * ROWS_W + first, 16), size)]
        return push(weight.at[:, pl.ds(first, size)], mine, sem_w, slot + d, at(dx=d))

    wx = [
        [some_rows(d, 0, EARLY_W, 0) for d in range(1, NX)],
        [some_rows(d, EARLY_W, ROWS_W - EARLY_W, 3 * NX) for d in range(1, NX)],
    ]
    wz = [
        push(weight.at[:, pl.ds(first, size)], w_all.at[:, pl.ds(pl.multiple_of(line * ROWS_W + first, 16), size)], sem_w, slot, at(dz=1))
        for first, size, slot in ((0, CUT_W, 0), (CUT_W, ROWS_W - CUT_W, 3 * NX))
    ]
    for copy in in_key:
        copy.wait()
    start(kx + own_kz + wz[:1])
    beside = w_all.at[:, pl.ds(pl.multiple_of((x * NZ + 1 - zh) * ROWS_W, 16), CUT_W)]
    on_x = [push(beside, beside, sem_w, NX + d, at(dx=d)) for d in range(1, NX)]
    on_z = []
    for d in range(1, NX):
        first = lax.rem(x - d + NX, NX) * NZ + zh
        below = w_all.at[:, pl.ds(pl.multiple_of(first * ROWS_W + CUT_W, 16), ROWS_W - CUT_W)]
        on_z.append(push(below, below, sem_w, 2 * NX + d, at(dz=1)))

    halo_wait(f_made, f_got, sem_hf)
    for k, first, size in lanes:
        span = slice(first, first + size)
        gf[k, :, 0, 0, 8:24, :size] = fr_row[0, :, :, span]
        gf[k, :, 16, 1, 8:24, :size] = fr_row[1, :, :, span]
        for side, col in ((0, 7), (1, 24)):
            gf[k, :, 0:16, 1, col : col + 1, :size] = fr_col[side, :, :, 0, :, span]
            gf[k, :, 1:17, 0, col : col + 1, :size] = fr_col[side, :, :, 1, :, span]
            gf[k, :, 0, 0, col : col + 1, :size] = fr_cor[side, :, :, span]
            gf[k, :, 16, 1, col : col + 1, :size] = fr_cor[2 + side, :, :, span]
        for f in range(2):
            four = [gf[k, f, :, :, pl.ds(7 + s, 8, stride=2), :][..., :size] for s in range(4)]
            for tap in range(3):
                vf[tap, f, :, :, :, span] = four[2 - tap] + four[3 - tap]
    in_up.wait()

    def causal(cells, weights, dims):
        own = later = None
        for tap in range(9):
            both = jnp.concatenate([cells(0, tap), cells(1, tap)], axis=0)
            one = mm(both, weights[1, tap], dims)
            two = mm(both[TOK:], weights[0, tap], dims)
            own = one if own is None else own + one
            later = two if later is None else later + two
        return own[:TOK] + later, own[TOK:]

    def fine_cells(f, tap):
        b, col = tap // 3, tap % 3
        one = vf[col, f, 0:16, 1] if b else vf[col, f, 1:17, 0]
        two = (vf[col, f, 1:17, 1], vf[col, f, 1:17, 0], vf[col, f, 0:16, 0])[b]
        return (one + two).reshape(TOK, FINE).astype(BF)

    scale = gain[...].reshape(1, CH)
    for f, pooled in enumerate(causal(fine_cells, uw, NN)):
        z = scale * wide(preact[f].reshape(TOK, CH))
        s = 1.0 / (1.0 + jnp.exp(-z))
        mid = (pooled * scale * s * (1.0 + z * (1.0 - s))).astype(BF)
        mf[f, 1:17, 8:16, :] = wide(mid).reshape(16, 8, CH)
    ms_row[0] = mf[:, 1, 8:16, :]
    ms_row[1] = mf[:, 16, 8:16, :]
    for side, col in ((0, 8), (1, 15)):
        ms_col[side] = mf[:, 1:17, col : col + 1, :]
        ms_cor[side] = mf[:, 1, col : col + 1, :]
        ms_cor[2 + side] = mf[:, 16, col : col + 1, :]
    m_made = [ms_row.at[0], ms_row.at[1], ms_col.at[0], ms_col.at[1]] + [ms_cor.at[i] for i in range(4)]
    m_got = [mr_row.at[0], mr_row.at[1], mr_col.at[0], mr_col.at[1]] + [mr_cor.at[i] for i in range(4)]
    halo_start(m_made, m_got, sem_hm)
    arrived(kx)
    start(kz + to_q + vx + [wx[0][0], wx[0][2]])
    in_mid.wait()
    halo_wait(m_made, m_got, sem_hm)
    mf[:, 0, 8:16, :] = mr_row[0]
    mf[:, 17, 8:16, :] = mr_row[1]
    for side, col in ((0, 7), (1, 16)):
        mf[:, 1:17, col : col + 1, :] = mr_col[side]
        mf[:, 0, col : col + 1, :] = mr_cor[side]
        mf[:, 17, col : col + 1, :] = mr_cor[2 + side]

    def mid_cells(f, tap):
        b, col = tap // 3, tap % 3
        return mf[f, 2 - b : 18 - b, 9 - col : 17 - col, :].reshape(TOK, CH).astype(BF)

    for f, total in enumerate(causal(mid_cells, mw, NT)):
        low = total.astype(BF)
        feature[f] = low.reshape(16, 8, CH)
        for k in range(3):
            ff[k, f] = wide(low[:, k * HEAD_DIM : (k + 1) * HEAD_DIM]).reshape(16, 8, HEAD_DIM)
    for t in range(2):
        for u in range(2):
            for w in range(2):
                first = ((t * 2 + u) * 2 + w) * CH
                for k in range(3):
                    span = slice(first + k * HEAD_DIM, first + (k + 1) * HEAD_DIM)
                    for p in range(8):
                        ps[p * 4 : p * 4 + 4, span] = ff[k, t, 2 * p + u, pl.ds(w, 4, stride=2), :]
    p_all[rows(c, 32), :] = ps[...].astype(BF)
    start(to_p)

    arrived(to_p[:1])
    start(on_p)
    for copy in in_rest + [in_patch, in_weight]:
        copy.wait()
    arrived(vx)
    start(own_vz + vz + wz[1:])
    arrived(to_p[1:] + on_p)
    g_own[...] = mm(p_all[...], pw[...]).astype(BF)
    to_g = to_queries(g_own, g_all, sem_g)
    start(to_g)
    start([wx[1][0], wx[1][2]])
    g_all[rows(plane), :] = g_own[:, cols(x)]
    g_all[rows(y, base=FULL), :] = g_own[:, cols(NX)]

    arrived(kz + own_kz + to_q)

    def spans(i):
        return rows(i, CHUNK), rows(i // FULL_CHUNKS, KEYS)

    def score_step(i, _):
        span, keys = spans(i)
        s = mm(k_all[keys, :], q_all[span, :], NT) * (FACTOR * LOG2E)
        peak = jnp.max(s, axis=0, keepdims=True)
        e = jnp.exp2(s - peak)
        stat_s[0, :, span] = peak
        stat_s[1, :, span] = jnp.sum(e, axis=0, keepdims=True)
        probs[:, span] = e.astype(BF)
        return 0

    lax.fori_loop(0, CHUNKS, score_step, 0, unroll=2)
    to_st = [push(stat_s, stat_r.at[y], sem_st, d, at(dy=d)) for d in range(1, NY)]
    start(to_st)
    stat_r[y] = stat_s[...]
    arrived(to_st)

    def share_step(i, _):
        span, _ = spans(i)
        top = stat_r[0, 0, :, span]
        for j in range(1, NY):
            top = jnp.maximum(top, stat_r[j, 0, :, span])
        total = jnp.zeros_like(top)
        for j in range(NY):
            total = total + stat_r[j, 1, :, span] * jnp.exp2(stat_r[j, 0, :, span] - top)
        share = jnp.exp2(stat_s[0, :, span] - top) / total
        probs[:, span] = (wide(probs[:, span]) * share).astype(BF)
        return 0

    lax.fori_loop(0, CHUNKS, share_step, 0, unroll=2)
    arrived(vz + own_vz + to_g)

    def grad_step(i, _):
        span, keys = spans(i)
        g = mm(v_all[keys, :], g_all[span, :], NT)
        dot_s[:, span] = jnp.sum(wide(probs[:, span]) * g, axis=0, keepdims=True)
        gp[:, span] = g.astype(BF)
        return 0

    lax.fori_loop(0, CHUNKS, grad_step, 0, unroll=2)
    to_rd = [push(dot_s, dot_r.at[y], sem_rd, d, at(dy=d)) for d in range(1, NY)]
    start(to_rd)
    dot_r[y] = dot_s[...]

    def key_copies(d, made, got, sems):
        copies = []
        block = lax.rem(x + d, NX) * NZ
        for dz in range(NZ):
            if d or dz:
                there = block + lax.rem(zh + dz, NZ)
                for k in range(2):
                    copies.append(
                        push(made.at[k, rows(there)], got.at[line, k], sems, 2 * (d * NZ + dz) + k, at(dx=d, dz=dz))
                    )
        return copies

    def key_sums(left, right, made, got, sems, scale):
        for d in (2, 1, 3, 0):
            block = rows(lax.rem(x + d, NX), NZ * TOK)
            made[0, block, :] = (scale * mm(left[block, :FULL], right[:FULL, :])).astype(BF)
            made[1, block, :] = (scale * mm(left[block, FULL:], right[FULL:, :])).astype(BF)
            start(key_copies(d, made, got, sems))
        got[line] = made[:, rows(line), :]

    def all_key_copies(made, got, sems):
        return [copy for d in range(NX) for copy in key_copies(d, made, got, sems)]

    key_sums(probs, g_all, dv_s, dv_r, sem_dv, 1.0)
    to_dv = all_key_copies(dv_s, dv_r, sem_dv)
    arrived(to_rd)

    def query_copies(d):
        copies = []
        there = lax.rem(y + d, NY)
        for dx in range(NX):
            if d or dx:
                block = rows(there * NX + lax.rem(x + dx, NX))
                copies.append(push(dq_s.at[block], dq_r.at[plane], sem_dq, d * NX + dx, at(dy=d, dx=dx)))
        return copies

    def last_copy(d):
        block = rows(lax.rem(y + d, NY), base=FULL)
        return push(dq_s.at[block], dl_r.at[y], sem_dq, NY * NX + d, at(dy=d))

    def query_step(i, _):
        span, keys = spans(i)
        dot = dot_r[0, :, span]
        for j in range(1, NY):
            dot = dot + dot_r[j, :, span]
        ds = (wide(probs[:, span]) * (wide(gp[:, span]) - dot)).astype(BF)
        gp[:, span] = ds
        dq_s[span, :] = (FACTOR * mm(ds, k_all[keys, :], TN)).astype(BF)
        return 0

    for d in (2, 1, 3, 0):
        first = lax.rem(y + d, NY) * 2
        query_step(first, 0)
        query_step(first + 1, 0)
        start(query_copies(d))
    query_step(FULL_CHUNKS, 0)
    query_step(FULL_CHUNKS + 1, 0)
    to_dl = [last_copy(d) for d in range(1, NY)]
    start(to_dl)
    dq_r[plane] = dq_s[rows(plane), :]
    dl_r[y] = dq_s[rows(y, base=FULL), :]
    key_sums(gp, q_all, dk_s, dk_r, sem_dk, FACTOR)
    to_dk = all_key_copies(dk_s, dk_r, sem_dk)
    arrived(wz[:1])
    start([wx[0][1], wx[1][1]] + on_x)
    to_dq = [copy for d in range(NY) for copy in query_copies(d)]

    def key_total(part_index, got):
        for h in range(NX):
            total = wide(got[h * NZ, 0])
            for j in range(1, NZ):
                total = total + wide(got[h * NZ + j, 0])
            a_all[part_index, rows(y), h * HEAD_DIM : (h + 1) * HEAD_DIM] = total.astype(BF)
        total = wide(got[0, 1])
        for j in range(1, NK):
            total = total + wide(got[j, 1])
        a_all[part_index, rows(y), NX * HEAD_DIM :] = total.astype(BF)

    def a_copies(k):
        mine = a_all.at[k, rows(y)]
        return [push(mine, mine, sem_a, k * NY + d, at(dy=d)) for d in (1, 3)]

    def a_onward(k):
        half = TOK // 2
        up = a_all.at[k, pl.ds(pl.multiple_of(lax.rem(y + 3, NY) * TOK, half), half)]
        down = a_all.at[k, pl.ds(pl.multiple_of(lax.rem(y + 1, NY) * TOK + half, half), half)]
        return [push(up, up, sem_a, k * NY, at(dy=1)), push(down, down, sem_a, k * NY + 2, at(dy=3))]

    to_a = [a_copies(k) for k in range(3)]
    on_a = [a_onward(k) for k in range(3)]
    arrived(to_dv)
    key_total(2, dv_r)
    start(to_a[2])
    arrived([wx[0][0], wx[0][2], wx[1][0], wx[1][2]])
    start([on_z[0], on_z[2]])
    arrived(to_dq + to_dl)
    for h in range(NX):
        total = wide(dq_r[h])
        for j in range(1, NY):
            total = total + wide(dq_r[j * NX + h])
        a_all[0, rows(y), h * HEAD_DIM : (h + 1) * HEAD_DIM] = total.astype(BF)
    total = wide(dl_r[0])
    for j in range(1, NY):
        total = total + wide(dl_r[j])
    a_all[0, rows(y), NX * HEAD_DIM :] = total.astype(BF)
    start(to_a[0])
    arrived(to_a[2])
    start(on_a[2])
    arrived([wx[0][1], wx[1][1]])
    start([on_z[1]])
    arrived(to_dk)
    key_total(1, dk_r)
    start(to_a[1])
    arrived(to_a[0])
    start(on_a[0])
    arrived(to_a[1])
    start(on_a[1])
    for k in (2, 0, 1):
        arrived(on_a[k])
    arrived(wz[1:] + on_x + on_z)

    def project(first, size):
        span = pl.ds(pl.multiple_of(first, HEAD_DIM), size)
        total = mm(a_all[0], w_all[0, span, :], NT)
        total = total + mm(a_all[1], w_all[1, span, :], NT)
        return total + mm(a_all[2], w_all[2, span, :], NT)

    to_c = []
    def give(n):
        first, size = PIECES[n]
        part[:, first : first + size] = project((1 - core) * HALF + first, size).astype(BF)
        span = pl.ds(first, size)
        copy = push(part.at[:, span], pair.at[:, span], sem_c, n, partner)
        copy.start()
        to_c.append(copy)

    def out_copy(n, d):
        first, size = PIECES[n]
        to = lax.rem(y + d, NY)
        span = pl.ds(pl.multiple_of(core * HALF + first, HEAD_DIM), size)
        return push(
            pair.at[rows(to), pl.ds(first, size)], red.at[zl, :, span], sem_o, n * NY + d,
            (y // 2, lax.rem(y, 2), to, x, zh), n * NY + c,
        )

    def keep(n):
        first, size = PIECES[n]
        total = project(core * HALF + first, size)
        to_c[n].wait_recv()
        span = pl.ds(first, size)
        pair[:, span] = (total + wide(pair[:, span])).astype(BF)
        for d in (2, 1, 3):
            out_copy(n, d).start()

        @pl.when(c == y)
        def _():
            red[zl, :, pl.ds(pl.multiple_of(core * HALF + first, HEAD_DIM), size)] = pair[rows(y), span]

        @pl.when(c != y)
        def _():
            out_copy(n, 0).start()

    give(0)
    give(1)
    keep(0)
    give(2)
    keep(1)
    keep(2)

    done = to_p + on_p + wz + to_k + to_q + to_v + wx[0] + wx[1] + on_x + on_z + to_g + to_st + to_rd + to_dv + to_dq + to_dl + to_dk
    for copy in done + to_a[0] + to_a[1] + to_a[2] + on_a[0] + on_a[1] + on_a[2] + to_c:
        copy.wait_send()
    halo_wait(f_made, f_got, sem_hf, sent=True)
    halo_wait(m_made, m_got, sem_hm, sent=True)

    for n, (first, size) in enumerate(PIECES):
        for other in range(TY):
            @pl.when((c != y) | (c != other))
            def _():
                push(
                    pair.at[rows(0), pl.ds(first, size)], red.at[other // 2, :, pl.ds((other % 2) * HALF + first, size)],
                    sem_o, n * NY, at(dy=1), n * NY + other,
                ).wait_recv()
        for half in range(2):
            span = pl.ds(half * HALF + first, size)
            out[:, span] = (wide(red[0, :, span]) + wide(red[1, :, span])).astype(BF)

    for n in range(len(PIECES)):
        for d in range(1, NY):
            out_copy(n, d).wait_send()

        @pl.when(c != y)
        def _():
            out_copy(n, 0).wait_send()


def body(
    out_grad,
    preact,
    norm_gain,
    mid_weight,
    up_weight,
    patch_weight,
    query_proj,
    key_proj,
    value_proj,
    qkv_weight,
):
    any_space = pl.BlockSpec(memory_space=pl.ANY)

    def sems(count):
        return pltpu.SemaphoreType.DMA((2, count))

    in_vmem = pl.BlockSpec(memory_space=pltpu.VMEM)

    def strips(count, *shape):
        return pltpu.VMEM((count, 2) + shape, F32)

    return pl.pallas_call(
        whole_kernel,
        out_shape=(
            jax.ShapeDtypeStruct((2, 16, 8, CH), BF),
            jax.ShapeDtypeStruct((TOK, OUT), BF),
        ),
        in_specs=[any_space] + [in_vmem] * 2 + [any_space] * 7,
        out_specs=(in_vmem, in_vmem),
        scratch_shapes=[
            pltpu.VMEM((2, 16, 2, 16, FINE), BF),
            pltpu.VMEM((2, 2, 17, 2, 32, HEAD_DIM), F32),
            pltpu.VMEM((3, 2, 17, 2, 8, FINE), F32),
            pltpu.VMEM((2, 9, FINE, CH), BF),
            pltpu.VMEM((2, 9, CH, CH), BF),
            pltpu.VMEM((2, 18, 24, CH), F32),
            pltpu.VMEM((3, 2, 16, 8, HEAD_DIM), F32),
            pltpu.VMEM((32, PATCH), F32),
            strips(2, 16, FINE),
            strips(2, 16, 2, 1, FINE),
            strips(4, 1, FINE),
            strips(2, 16, FINE),
            strips(2, 16, 2, 1, FINE),
            strips(4, 1, FINE),
            strips(2, 8, CH),
            strips(2, 16, 1, CH),
            strips(4, 1, CH),
            strips(2, 8, CH),
            strips(2, 16, 1, CH),
            strips(4, 1, CH),
            sems(8),
            sems(8),
            pltpu.VMEM((TOK, PATCH), BF),
            pltpu.VMEM((PATCH, COLS), BF),
            pltpu.VMEM((QUERIES, HEAD_DIM), BF),
            pltpu.VMEM((2 * KEYS, HEAD_DIM), BF),
            pltpu.VMEM((2 * KEYS, HEAD_DIM), BF),
            pltpu.VMEM((TOK, COLS), BF),
            pltpu.VMEM((QUERIES, HEAD_DIM), BF),
            pltpu.VMEM((3, OUT, COLS), BF),
            pltpu.VMEM((KEYS, QUERIES), BF),
            pltpu.VMEM((KEYS, QUERIES), BF),
            pltpu.VMEM((2, 1, QUERIES), F32),
            pltpu.VMEM((NY, 2, 1, QUERIES), F32),
            pltpu.VMEM((1, QUERIES), F32),
            pltpu.VMEM((NY, 1, QUERIES), F32),
            pltpu.VMEM((QUERIES, HEAD_DIM), BF),
            pltpu.VMEM((NY * NX, TOK, HEAD_DIM), BF),
            pltpu.VMEM((NY, TOK, HEAD_DIM), BF),
            pltpu.VMEM((2, KEYS, HEAD_DIM), BF),
            pltpu.VMEM((NK, 2, TOK, HEAD_DIM), BF),
            pltpu.VMEM((2, KEYS, HEAD_DIM), BF),
            pltpu.VMEM((NK, 2, TOK, HEAD_DIM), BF),
            pltpu.VMEM((3, LAST, COLS), BF),
            pltpu.VMEM((LAST, HALF), BF),
            pltpu.VMEM((LAST, HALF), BF),
            pltpu.VMEM((2, TOK, OUT), BF),
            sems(TY),
            sems(NY * NX + NY),
            sems(2 * NK),
            sems(2 * NK),
            sems(4 * NX),
            sems(NY * NX + NY),
            sems(NY),
            sems(NY),
            sems(NY * NX + NY),
            sems(2 * NK),
            sems(2 * NK),
            sems(3 * NY),
            sems(len(PIECES)),
            sems(len(PIECES) * NY),
            pltpu.SemaphoreType.DMA((11,)),
        ],
        compiler_params=pltpu.CompilerParams(
            collective_id=0, has_side_effects=True, vmem_limit_bytes=56 * 1024 * 1024
        ),
        name="whole",
    )(
        out_grad.reshape(2, 16, 2, 16, FINE),
        preact,
        norm_gain,
        up_weight.transpose(0, 1, 2, 4, 3).reshape(3, 9, FINE, CH),
        mid_weight.reshape(3, 9, CH, CH),
        patch_weight,
        query_proj,
        key_proj,
        value_proj,
        qkv_weight.transpose(1, 0, 2),
    )


def solution(mesh):
    split = Mesh(mesh.devices.reshape(SIZES), AXES)
    ty, tx = ("zl", "core"), ("y", "x", "zh")
    placed = (
        P(None, ty, tx, None),
        P(None, ty, tx, None),
        P(),
        P(),
        P(),
        P(None, ty),
        P(tx, ty),
        P(tx, ty),
        P(tx, ty),
        P(tx, None, ty),
    )
    return jax.shard_map(
        body,
        mesh=split,
        in_specs=placed,
        out_specs=(P(None, ty, tx, None), P(tx, ty)),
        check_vma=False,
    )
```
